32 devices in a mesh: groups: 2 (over y), lon: 4 (over z), lat: 2 (over x), tm: 2 (over core).
Axes of the slice: x: 2, y: 2, z: 4, core: 2. Of those that a mesh axis runs over, the one named last changes fastest.
Arguments:
- kappa_squared: float32 [512, 1024], P('lat', 'lon'), may hold values from 0.05 to 1
- time_coupling: float32 [512, 1024], P('lat', 'lon'), may hold values from 0.3 to 0.95
- station_value: float32 [16384], P(('groups', 'lon', 'lat', 'tm')), parts along dimension 0, may hold values from -8 to 8
- station_weight: float32 [16384], P(('groups', 'lon', 'lat', 'tm')), parts along dimension 0, may hold values from 0.5 to 4
- station_cell: int32 [3, 16384], P(None, ('groups', 'lon', 'lat', 'tm')), parts along dimension 1, may hold values from 0 to 1023, as said below
- slab_blocks: int32 [8], P(('groups', 'lon')), parts along dimension 0, may hold values from 1 to 4, as said below
Outputs:
- kriged_field: float32 [16, 512, 1024], P(('groups', 'tm'), 'lat', 'lon'), parts along dimension 0
- station_fit: float32 [16384], P(('groups', 'lon', 'lat', 'tm')), parts along dimension 0
The draws below stay inside these ranges and needn't reach their ends.
There are 2 independent parts, one for each index of `groups`. The reference program is written for one: setup_inputs(seed, part) draws one part's arguments, and reference() takes and returns one part's arrays. A program takes and returns all parts, laid end to end along the dimension named above; an argument that names none is the same for every part. Nothing has to cross between parts.
Inputs may be any that keep to these rules, and one draw needn't show every extreme that they name: `station_cell`: rows are longitude, latitude, hour. A row held by a device of longitude slab s has longitude in s * 256 to (s + 1) * 256 - 1. Among each device's 512 rows, padding included, every pair of a latitude band of 256 latitudes and an hour group of 4 hours is named by exactly 128 rows. The longitude 1024 - 1 is named in every draw. Every device of slab s holds its live stations in its first 128 * slab_blocks[s] rows. Some slab is full.
All inputs are finite; a program needn't handle non-finite values.
Results may differ from the reference program's by a relative error of at most 0.0001.
Values sent between devices are 32-bit elements; how exact they have to be, the bound alone decides.
A program may use at most 64 MiB of HBM per device.

```python
import math
import jax
import jax.numpy as jnp

CLON = 256
CLAT = 256
HOURS = 8
ITERS = 2
BLOCK = 128
BLOCKS_DEV = 4
CH = 4
ST_DEV = 512
CAP = 128
SLAB_ROWS = 2048
STATIONS = 8192
NLON = 1024
NLAT = 512
N_LON = 4
N_LAT = 2
N_TM = 2


def draw_station_cell(key, part):
    key = jax.random.fold_in(key, 3)
    key_order, key_lon, key_lat, key_hour, key_edge, key_side = jax.random.split(key, 6)
    devices = N_LON * N_LAT * N_TM
    owners = N_LAT * N_TM
    scores = jax.random.randint(key_order, (devices, ST_DEV), 0, 1 << 20) * ST_DEV + jnp.arange(ST_DEV)[None, :]
    rank_order = jnp.argsort(scores, axis=1).astype(jnp.int32)
    owner_index = rank_order // CAP
    slab_index = (jnp.arange(devices) // owners)[:, None]
    longitude = slab_index * CLON + jax.random.randint(key_lon, (devices, ST_DEV), 0, CLON)
    last_row = (jnp.arange(devices)[:, None] == devices - 1) & (jnp.arange(ST_DEV)[None, :] == 0)
    longitude = jnp.where(last_row, N_LON * CLON - 1, longitude)
    spread_lat = jax.random.randint(key_lat, (devices, ST_DEV), 0, CLAT)
    edge_pick = jax.random.randint(key_edge, (devices, ST_DEV), 0, 4)
    edge_lat = jnp.where(edge_pick == 0, 0, jnp.where(edge_pick == 1, 1, jnp.where(edge_pick == 2, CLAT - 2, CLAT - 1)))
    near_edge = jax.random.randint(key_side, (devices, ST_DEV), 0, 2) == 1
    lat_offset = jnp.where(near_edge, edge_lat, spread_lat)
    latitude = owner_index // N_TM * CLAT + lat_offset
    hour_index = owner_index % N_TM * CH + jax.random.randint(key_hour, (devices, ST_DEV), 0, CH)
    stacked = jnp.stack([longitude, latitude, hour_index])
    return stacked.reshape(3, STATIONS).astype(jnp.int32)


def draw_slab_blocks(key, part):
    key = jax.random.fold_in(key, 5)
    key_count, key_full = jax.random.split(key)
    counts = jax.random.randint(key_count, (N_LON,), 1, BLOCKS_DEV + 1)
    full_slab = jax.random.randint(key_full, (), 0, N_LON)
    return jnp.where(jnp.arange(N_LON) == full_slab, BLOCKS_DEV, counts).astype(jnp.int32)


def draw_station_value(key, part):
    key = jax.random.fold_in(key, 7)
    row_index = jnp.arange(STATIONS)
    slab_index = (row_index // SLAB_ROWS).astype(jnp.float32)
    spread = 0.5 + 1.5 * slab_index / max(N_LON - 1, 1)
    noise = jnp.clip(jax.random.normal(key, (STATIONS,), jnp.float32), -4.0, 4.0)
    return (spread * noise).astype(jnp.float32)


def level_of(rng, shape, pieces, least, top_value):
    gain, own = 1.0, jax.random.fold_in(rng, 6)
    for axis_at, parts in pieces:
        steps = jnp.exp(jax.random.uniform(jax.random.fold_in(own, axis_at), (parts,), jnp.float32, least / len(pieces), top_value / len(pieces)))
        gain = gain * jnp.repeat(steps, shape[axis_at] // parts).reshape([-1 if axis == axis_at else 1 for axis in range(len(shape))])
    return gain


def setup_inputs(seed: int = 0, part: int = 0) -> dict:
    splits = jax.random.split(jax.random.key(seed), 7)
    own_keys = jax.random.split(jax.random.fold_in(splits[6], part), 7)
    kappa_squared = jnp.clip(jnp.exp(math.log(1.0) - 2.9957323 * jax.random.uniform(splits[0], (NLAT, NLON), jnp.float32) ** level_of(splits[0], (NLAT, NLON), ((0, 2), (1, 4)), -0.2, 0.2)), 0.05, 1.0)
    time_coupling = jnp.clip(0.3 + 0.65 * jax.random.uniform(splits[1], (NLAT, NLON), jnp.float32) ** level_of(splits[1], (NLAT, NLON), ((0, 2), (1, 4)), -0.2, 0.2), 0.3, 0.95)
    station_value = draw_station_value(jax.random.fold_in(jax.random.fold_in(splits[6], part), 71), part)
    station_weight = jnp.clip(jnp.exp(math.log(4.0) - 2.0794415 * jax.random.uniform(own_keys[3], (STATIONS,), jnp.float32) ** level_of(own_keys[3], (STATIONS,), ((0, 16),), -0.2, 0.2)), 0.5, 4.0)
    station_cell = draw_station_cell(jax.random.fold_in(jax.random.fold_in(splits[6], part), 71), part)
    slab_blocks = draw_slab_blocks(jax.random.fold_in(jax.random.fold_in(splits[6], part), 71), part)
    return {"kappa_squared": kappa_squared, "time_coupling": time_coupling, "station_value": station_value, "station_weight": station_weight, "station_cell": station_cell, "slab_blocks": slab_blocks}


def stiffen_grid(values_in, kappa_squared):
    padded = jnp.pad(values_in, ((0, 0), (1, 1), (0, 0)))
    beside_all = padded[:, 2:, :] + padded[:, :-2, :] + jnp.roll(values_in, 1, axis=2) + jnp.roll(values_in, -1, axis=2)
    return (kappa_squared + 1.0) * values_in - 0.25 * beside_all


def couple_hours(values_in, time_coupling):
    padded = jnp.pad(values_in, ((1, 1), (0, 0), (0, 0)))
    hour_index = jnp.arange(values_in.shape[0])
    at_edge = (hour_index == 0) | (hour_index == values_in.shape[0] - 1)
    diagonal = jnp.where(at_edge[:, None, None], jnp.ones_like(time_coupling), 1.0 + time_coupling * time_coupling)
    return diagonal * values_in - time_coupling * (padded[2:] + padded[:-2])


def reference(kappa_squared, time_coupling, station_value, station_weight, station_cell, slab_blocks):
    lat_total, lon_total = kappa_squared.shape
    grid_shape = (HOURS, lat_total, lon_total)
    row_index = jnp.arange(STATIONS, dtype=jnp.int32)
    slab_index = (row_index // SLAB_ROWS).astype(jnp.int32)
    is_live = (row_index % ST_DEV) < slab_blocks[slab_index] * BLOCK
    flat_cell = ((station_cell[2] * lat_total + station_cell[1]) * lon_total + station_cell[0]).astype(jnp.int32)
    weights = jnp.where(is_live, station_weight, jnp.zeros_like(station_weight))
    cell_total = HOURS * lat_total * lon_total
    observed = jnp.zeros(cell_total, jnp.float32).at[flat_cell].add(weights).reshape(grid_shape)
    right_side = jnp.zeros(cell_total, jnp.float32).at[flat_cell].add(weights * station_value).reshape(grid_shape)

    def precision(values_in):
        inner_term = couple_hours(stiffen_grid(values_in, kappa_squared), time_coupling)
        return stiffen_grid(inner_term, kappa_squared) + observed * values_in

    solution = jnp.zeros(grid_shape, jnp.float32)
    residual = right_side
    direction = right_side
    norm_now = jnp.sum(residual * residual)
    for iteration in range(ITERS):
        applied = precision(direction)
        step_length = norm_now / jnp.sum(direction * applied)
        solution = solution + step_length * direction
        if iteration + 1 < ITERS:
            residual = residual - step_length * applied
            norm_next = jnp.sum(residual * residual)
            direction = residual + (norm_next / norm_now) * direction
            norm_now = norm_next
    picked = solution.reshape(-1)[flat_cell]
    station_fit = jnp.where(is_live, picked, jnp.zeros_like(picked))
    return solution, station_fit
```

```python
import functools

import jax
import jax.numpy as jnp
from jax import lax
from jax.experimental import pallas as pl
from jax.experimental.pallas import tpu as pltpu
from jax.sharding import PartitionSpec as P

HOURS = 8
BLOCK = 128
PAD = 8
ROWS = 64
LANES = 128
MESH = pl.DeviceIdType.MESH
F32 = jnp.float32
BF16 = jnp.bfloat16
NT = (((1,), (1,)), ((), ()))


def split(value):
    high = value.astype(BF16)
    return high, (value - high.astype(F32)).astype(BF16)


def dot(left, right, dims=None):
    if dims is None:
        return jnp.dot(left, right, preferred_element_type=F32)
    return lax.dot_general(left, right, dims, preferred_element_type=F32)


def fold(chunk):
    rows, cols = chunk.shape
    summed = jnp.sum(chunk.reshape(rows // 8, 8, cols), axis=0)
    total = summed[:, :LANES]
    for first in range(LANES, cols, LANES):
        total = total + summed[:, first : first + LANES]
    return total


def kernel(
    sizes,
    kappa_ref,
    tau_ref,
    value_ref,
    weight_ref,
    cell_ref,
    blocks_ref,
    field_ref,
    fit_ref,
    start_buf,
    image_buf,
    stiff_buf,
    couple_buf,
    second_buf,
    observed_buf,
    row_hot,
    lon_hot,
    slot_hot,
    station_out,
    station_in,
    back_out,
    back_in,
    edge_out,
    edge_in,
    columns,
    sum_out,
    sum_in,
    station_send,
    station_recv,
    back_send,
    back_recv,
    edge_send,
    edge_recv,
    plane_send,
    plane_recv,
    sum_send,
    sum_recv,
):
    n_lon, n_lat, n_tm, hours, lats, lons, stations, padded = sizes
    owners = n_lat * n_tm
    capacity = stations // owners
    slots = owners * padded
    members = n_lon * owners
    lon, lat, tm = lax.axis_index("lon"), lax.axis_index("lat"), lax.axis_index("tm")
    owner = lat * n_tm + tm
    member = lon * owners + owner
    edge_hour = jnp.where(tm == 0, hours - 1, 0)
    chunks = range(0, lats, ROWS)

    def place(index):
        return {
            "lon": lax.div(index, owners),
            "lat": lax.rem(lax.div(index, n_tm), n_lat),
            "tm": lax.rem(index, n_tm),
        }

    def place_owner(index):
        return {"lon": lon, "lat": lax.div(index, n_tm), "tm": lax.rem(index, n_tm)}

    barrier = pltpu.get_barrier_semaphore()

    def greet(step, carry):
        pl.semaphore_signal(
            barrier, inc=1, device_id=place(lax.rem(member + step, members)), device_id_type=MESH
        )
        return carry

    lax.fori_loop(1, members, greet, 0)

    live = lax.broadcasted_iota(jnp.int32, (1, stations), 1) < blocks_ref[0] * BLOCK
    weight = jnp.where(live, weight_ref[...], 0.0)
    lon_at, lat_at, hour_at = cell_ref[0:1, :], cell_ref[1:2, :], cell_ref[2:3, :]
    own_lat = jnp.zeros_like(lat_at)
    for band in range(1, n_lat):
        own_lat = own_lat + (lat_at >= band * lats).astype(jnp.int32)
    own_tm = jnp.zeros_like(lat_at)
    for group in range(1, n_tm):
        own_tm = own_tm + (hour_at >= group * hours).astype(jnp.int32)
    away = own_lat * n_tm + own_tm - owner
    away = jnp.where(away < 0, away + owners, away)
    row_at = (hour_at - own_tm * hours) * lats + lat_at - own_lat * lats
    col_at = lon_at - lon * lons
    kinds = max(16, owners)
    hot = lax.broadcasted_iota(jnp.int32, (kinds, stations), 0) == away
    earlier = lax.broadcasted_iota(jnp.int32, (stations, stations), 0) < lax.broadcasted_iota(
        jnp.int32, (stations, stations), 1
    )
    counts = dot(hot.astype(F32).astype(BF16), earlier.astype(F32).astype(BF16))
    rank = jnp.sum(jnp.where(hot, counts, 0.0), axis=0, keepdims=True).astype(jnp.int32)
    slot = away * padded + rank
    slot_hot[...] = (
        (lax.broadcasted_iota(jnp.int32, (slots, stations), 0) == slot).astype(F32).astype(BF16)
    )
    payload = jnp.concatenate(
        [
            weight,
            weight * value_ref[...],
            row_at.astype(F32),
            col_at.astype(F32),
            jnp.zeros((4, stations), F32),
        ],
        axis=0,
    )
    high, low = split(payload)
    both = dot(jnp.concatenate([high, low], axis=0), slot_hot[...], NT)
    packed = both[:8] + both[8:]
    for step in range(owners):
        chunk = packed[:, step * padded : (step + 1) * padded]
        if step == 0:
            station_in[owners - 1] = chunk
        else:
            station_out[step - 1] = chunk

    pl.semaphore_wait(barrier, members - 1)

    def station_copy(step):
        return pltpu.make_async_remote_copy(
            src_ref=station_out.at[step - 1],
            dst_ref=station_in.at[step - 1],
            send_sem=station_send.at[step - 1],
            recv_sem=station_recv.at[step - 1],
            device_id=place_owner(lax.rem(owner + step, owners)),
            device_id_type=MESH,
        )

    for step in range(1, owners):
        station_copy(step).start()
    for step in range(1, owners):
        station_copy(step).wait()

    arrived = jnp.concatenate([station_in[index] for index in range(owners)], axis=1)
    here_row = arrived[2:3].astype(jnp.int32)
    here_col = arrived[3:4].astype(jnp.int32)
    cells = hours * lats
    row_hot[...] = (
        (lax.broadcasted_iota(jnp.int32, (cells, slots), 0) == here_row).astype(F32).astype(BF16)
    )
    col_mask = lax.broadcasted_iota(jnp.int32, (lons, slots), 0) == here_col
    lon_hot[...] = col_mask.astype(F32).astype(BF16)

    def spread(quantity):
        high, low = split(jnp.where(col_mask, quantity, 0.0))
        return high, low

    weight_high, weight_low = spread(arrived[0:1])
    right_high, right_low = spread(arrived[1:2])

    for hour in range(hours):
        hot_rows = row_hot[hour * lats : (hour + 1) * lats, :]
        start_buf[hour, PAD : PAD + lats, :] = dot(hot_rows, right_high, NT) + dot(
            hot_rows, right_low, NT
        )

    lane = lax.broadcasted_iota(jnp.int32, (ROWS, lons), 1)
    lon_up, lon_down = lax.rem(lon + 1, n_lon), lax.rem(lon + n_lon - 1, n_lon)
    lat_up, lat_down = lax.rem(lat + 1, n_lat), lax.rem(lat + n_lat - 1, n_lat)
    lat_ways = 1 if n_lat == 2 else 2
    pair = lax.rem(tm + 1, n_tm)

    def edge_copies(phase, wide):
        copies = []
        ways = [(0, lon_up, lat), (0, lon_down, lat), (1, lon, lat_up), (1, lon, lat_down)]
        for across in range(2 if wide else 1):
            for way in range(2 + lat_ways):
                tile, to_lon, to_lat = ways[way]
                index = across * 4 + way
                copies.append(
                    pltpu.make_async_remote_copy(
                        src_ref=edge_out.at[phase, tile],
                        dst_ref=edge_in.at[phase, index],
                        send_sem=edge_send.at[phase, index],
                        recv_sem=edge_recv.at[phase, index],
                        device_id={"lon": to_lon, "lat": to_lat, "tm": pair if across else tm},
                        device_id_type=MESH,
                    )
                )
        return copies

    def plane_copy(ref, which):
        return pltpu.make_async_remote_copy(
            src_ref=ref.at[edge_hour, pl.ds(PAD, lats)],
            dst_ref=ref.at[hours, pl.ds(PAD, lats)],
            send_sem=plane_send.at[which],
            recv_sem=plane_recv.at[which],
            device_id={"lon": lon, "lat": lat, "tm": pair},
            device_id_type=MESH,
        )

    def send_edges(ref, phase, wide):
        last = [ref[hour, PAD : PAD + lats, lons - 1 : lons] for hour in range(hours)]
        first = [ref[hour, PAD : PAD + lats, 0:1] for hour in range(hours)]
        beside = jnp.concatenate(
            last + first + [jnp.zeros((lats, LANES - 2 * hours), F32)], axis=1
        )
        edge_out[phase, 0] = beside.T[: 2 * hours]
        edge_out[phase, 1] = jnp.concatenate(
            [ref[hour, PAD + lats - 1 : PAD + lats, :] for hour in range(hours)]
            + [ref[hour, PAD : PAD + 1, :] for hour in range(hours)],
            axis=0,
        )
        for copy in edge_copies(phase, wide):
            copy.start()

    def take_edges(ref, phase, wide):
        for copy in edge_copies(phase, wide):
            copy.wait()
        tiles = [edge_in[phase, index] for index in (0, 1)]
        if wide:
            tiles += [edge_in[phase, index] for index in (4, 5)]
        stacked = jnp.concatenate(
            tiles + [jnp.zeros((LANES - 2 * hours * len(tiles), lats), F32)], axis=0
        )
        columns[...] = stacked.T
        below = edge_in[phase, 2]
        above = edge_in[phase, 1 + lat_ways]
        for hour in range(hours):
            ref[hour, PAD - 1 : PAD, :] = jnp.where(lat == 0, 0.0, below[hour : hour + 1])
            ref[hour, PAD + lats : PAD + lats + 1, :] = jnp.where(
                lat == n_lat - 1, 0.0, above[hours + hour : hours + hour + 1]
            )
        if wide:
            below = edge_in[phase, 6]
            above = edge_in[phase, 5 + lat_ways]
            below = jnp.where(tm == 0, below[0:1], below[hours - 1 : hours])
            above = jnp.where(tm == 0, above[hours : hours + 1], above[2 * hours - 1 :])
            ref[hours, PAD - 1 : PAD, :] = jnp.where(lat == 0, 0.0, below)
            ref[hours, PAD + lats : PAD + lats + 1, :] = jnp.where(lat == n_lat - 1, 0.0, above)

    def stiffen(ref, hour, row):
        centre = ref[hour, PAD + row : PAD + row + ROWS, :]
        rows = slice(row, row + ROWS)
        if hour < hours:
            left = columns[rows, hour : hour + 1]
            right = columns[rows, 3 * hours + hour : 3 * hours + hour + 1]
        else:
            at = 4 * hours
            left = jnp.where(
                tm == 0, columns[rows, at : at + 1], columns[rows, at + hours - 1 : at + hours]
            )
            at = 7 * hours
            right = jnp.where(
                tm == 0, columns[rows, at : at + 1], columns[rows, at + hours - 1 : at + hours]
            )
        beside = (
            jnp.where(lane == 0, left, pltpu.roll(centre, 1, 1))
            + jnp.where(lane == lons - 1, right, pltpu.roll(centre, lons - 1, 1))
            + ref[hour, PAD + row - 1 : PAD + row - 1 + ROWS, :]
            + ref[hour, PAD + row + 1 : PAD + row + 1 + ROWS, :]
        )
        return (kappa_ref[rows, :] + 1.0) * centre - 0.25 * beside

    def couple(row):
        rows = slice(row, row + ROWS)
        tau = tau_ref[rows, :]
        inner = 1.0 + tau * tau
        plane = [stiff_buf[hour, rows, :] for hour in range(hours + 1)]
        for hour in range(hours):
            if hour == 0:
                below = jnp.where(tm == 0, 0.0, plane[hours])
                diagonal = jnp.where(tm == 0, 1.0, inner)
            else:
                below = plane[hour - 1]
                diagonal = inner
            if hour == hours - 1:
                above = jnp.where(tm == n_tm - 1, 0.0, plane[hours])
                diagonal = jnp.where(tm == n_tm - 1, 1.0, inner)
            else:
                above = plane[hour + 1]
            couple_buf[hour, PAD + row : PAD + row + ROWS, :] = diagonal * plane[hour] - tau * (
                below + above
            )

    def sum_start(which, partial):
        sum_out[which] = jnp.sum(partial, axis=0, keepdims=True)

        def send(step, carry):
            pltpu.make_async_remote_copy(
                src_ref=sum_out.at[which],
                dst_ref=sum_in.at[which, step - 1],
                send_sem=sum_send.at[which],
                recv_sem=sum_recv.at[which],
                device_id=place(lax.rem(member + step, members)),
                device_id_type=MESH,
            ).start()
            return carry

        if members <= 16:
            for step in range(1, members):
                send(step, 0)
        else:
            lax.fori_loop(1, members, send, 0)

    def sum_finish(which):
        pltpu.make_async_remote_copy(
            src_ref=sum_in.at[which],
            dst_ref=sum_in.at[which],
            send_sem=sum_send.at[which],
            recv_sem=sum_recv.at[which],
            device_id=place(lax.rem(member + 1, members)),
            device_id_type=MESH,
        ).wait()
        total = jnp.sum(sum_in[which], axis=0) + sum_out[which]
        return jnp.sum(total, axis=1, keepdims=True)

    def gather(ref):
        picked = jnp.zeros((1, slots), F32)
        for hour in range(hours):
            high, low = split(ref[hour, PAD : PAD + lats, :])
            found = dot(high, lon_hot[...]) + dot(low, lon_hot[...])
            hot_rows = row_hot[hour * lats : (hour + 1) * lats, :].astype(F32)
            picked = picked + jnp.sum(found * hot_rows, axis=0, keepdims=True)
        return picked

    plane_copy(start_buf, 0).start()
    send_edges(start_buf, 0, True)
    for hour in range(hours):
        hot_rows = row_hot[hour * lats : (hour + 1) * lats, :]
        observed_buf[hour] = dot(hot_rows, weight_high, NT) + dot(hot_rows, weight_low, NT)
    norm_part = jnp.zeros((8, LANES), F32)
    for hour in range(hours):
        for row in chunks:
            chunk = start_buf[hour, PAD + row : PAD + row + ROWS, :]
            norm_part = norm_part + fold(chunk * chunk)
    sum_start(0, norm_part)
    picked_start = gather(start_buf)

    def image(source, target, base, phase, which):
        plane_copy(source, which).wait()
        take_edges(source, phase, True)
        for hour in range(hours + 1):
            for row in chunks:
                stiff_buf[hour, row : row + ROWS, :] = stiffen(source, hour, row)
        for row in chunks:
            couple(row)
        send_edges(couple_buf, phase + 1, False)
        take_edges(couple_buf, phase + 1, False)
        part = jnp.zeros((8, LANES), F32)
        for hour in range(hours):
            for row in chunks:
                at = slice(base + row, base + row + ROWS)
                own = source[hour, PAD + row : PAD + row + ROWS, :]
                result = (
                    stiffen(couple_buf, hour, row)
                    + observed_buf[hour, row : row + ROWS, :] * own
                )
                target[hour, at, :] = result
                if which == 0:
                    part = part + fold(own * result)
        return part

    part = image(start_buf, image_buf, PAD, 0, 0)
    plane_copy(image_buf, 1).start()
    send_edges(image_buf, 2, True)
    sum_start(1, part)
    image(image_buf, second_buf, 0, 2, 1)

    norm = sum_finish(0)
    step_first = norm / sum_finish(1)
    part = jnp.zeros((8, LANES), F32)
    for hour in range(hours):
        for row in chunks:
            at = slice(PAD + row, PAD + row + ROWS)
            rest = start_buf[hour, at, :] - step_first * image_buf[hour, at, :]
            couple_buf[hour, at, :] = rest
            part = part + fold(rest * rest)
    sum_start(2, part)
    ratio = sum_finish(2)
    norm_next = ratio
    ratio = ratio / norm
    part = jnp.zeros((8, LANES), F32)
    for hour in range(hours):
        for row in chunks:
            at = slice(PAD + row, PAD + row + ROWS)
            applied = image_buf[hour, at, :]
            direction = couple_buf[hour, at, :] + ratio * start_buf[hour, at, :]
            turned = (
                applied - step_first * second_buf[hour, row : row + ROWS, :] + ratio * applied
            )
            couple_buf[hour, at, :] = direction
            part = part + fold(direction * turned)
    sum_start(3, part)

    picked = jnp.concatenate(
        [picked_start, gather(couple_buf), jnp.zeros((6, slots), F32)], axis=0
    )
    for step in range(1, owners + 1):
        chunk = picked[:, (step - 1) * padded : step * padded]
        if step == owners:
            back_in[0] = chunk
        else:
            back_out[step - 1] = chunk

    def back_copy(step):
        return pltpu.make_async_remote_copy(
            src_ref=back_out.at[step - 1],
            dst_ref=back_in.at[step],
            send_sem=back_send.at[step - 1],
            recv_sem=back_recv.at[step - 1],
            device_id=place_owner(lax.rem(owner + owners - step, owners)),
            device_id_type=MESH,
        )

    for step in range(1, owners):
        back_copy(step).start()
    for step in range(1, owners):
        back_copy(step).wait()
    returned = jnp.concatenate([back_in[index] for index in range(owners)], axis=1)
    high, low = split(returned)
    both = dot(jnp.concatenate([high, low], axis=0), slot_hot[...])
    fitted = both[:8] + both[8:]

    step_second = norm_next / sum_finish(3)
    for hour in range(hours):
        for row in chunks:
            at = slice(PAD + row, PAD + row + ROWS)
            field_ref[hour, row : row + ROWS, :] = (
                step_first * start_buf[hour, at, :] + step_second * couple_buf[hour, at, :]
            )
    fit_ref[...] = jnp.where(live, step_first * fitted[0:1] + step_second * fitted[1:2], 0.0)


def body(kappa_squared, time_coupling, station_value, station_weight, station_cell, slab_blocks):
    n_lon, n_lat, n_tm = (lax.axis_size(axis) for axis in ("lon", "lat", "tm"))
    lats, lons = kappa_squared.shape
    stations = station_value.shape[0]
    hours = HOURS // n_tm
    owners = n_lat * n_tm
    members = n_lon * owners
    padded = -(-(stations // owners) // LANES) * LANES
    slots = owners * padded
    sizes = (n_lon, n_lat, n_tm, hours, lats, lons, stations, padded)
    tall = lats + 2 * PAD
    vmem = pl.BlockSpec(memory_space=pltpu.VMEM)
    dma = pltpu.SemaphoreType.DMA
    field, fit = pl.pallas_call(
        functools.partial(kernel, sizes),
        out_shape=(
            jax.ShapeDtypeStruct((hours, lats, lons), F32),
            jax.ShapeDtypeStruct((1, stations), F32),
        ),
        in_specs=[vmem] * 5 + [pl.BlockSpec(memory_space=pltpu.SMEM)],
        out_specs=(vmem, vmem),
        scratch_shapes=[
            pltpu.VMEM((hours + 1, tall, lons), F32),
            pltpu.VMEM((hours + 1, tall, lons), F32),
            pltpu.VMEM((hours + 1, lats, lons), F32),
            pltpu.VMEM((hours, tall, lons), F32),
            pltpu.VMEM((hours, lats, lons), F32),
            pltpu.VMEM((hours, lats, lons), F32),
            pltpu.VMEM((hours * lats, slots), BF16),
            pltpu.VMEM((lons, slots), BF16),
            pltpu.VMEM((slots, stations), BF16),
            pltpu.VMEM((owners - 1, 8, padded), F32),
            pltpu.VMEM((owners, 8, padded), F32),
            pltpu.VMEM((owners - 1, 8, padded), F32),
            pltpu.VMEM((owners, 8, padded), F32),
            pltpu.VMEM((4, 2, 2 * hours, lats), F32),
            pltpu.VMEM((4, 8, 2 * hours, lats), F32),
            pltpu.VMEM((lats, LANES), F32),
            pltpu.VMEM((4, 1, LANES), F32),
            pltpu.VMEM((4, members - 1, 1, LANES), F32),
            dma((owners - 1,)),
            dma((owners - 1,)),
            dma((owners - 1,)),
            dma((owners - 1,)),
            dma((4, 8)),
            dma((4, 8)),
            dma((2,)),
            dma((2,)),
            dma((4,)),
            dma((4,)),
        ],
        compiler_params=pltpu.CompilerParams(
            collective_id=0, has_side_effects=True, vmem_limit_bytes=48 * 1024 * 1024
        ),
    )(
        kappa_squared,
        time_coupling,
        station_value.reshape(1, stations),
        station_weight.reshape(1, stations),
        station_cell,
        slab_blocks,
    )
    return field, fit.reshape(stations)


def solution(mesh):
    rows = P(("groups", "lon", "lat", "tm"))
    return jax.shard_map(
        body,
        mesh=mesh,
        in_specs=(
            P("lat", "lon"),
            P("lat", "lon"),
            rows,
            rows,
            P(None, ("groups", "lon", "lat", "tm")),
            P(("groups", "lon")),
        ),
        out_specs=(P(("groups", "tm"), "lat", "lon"), rows),
        check_vma=False,
    )
```

```python
import functools

import jax
import jax.numpy as jnp
from jax import lax
from jax.experimental import pallas as pl
from jax.experimental.pallas import tpu as pltpu
from jax.sharding import PartitionSpec as P

HOURS = 8
BLOCK = 128
PAD = 8
ROWS = 64
LANES = 128
MESH = pl.DeviceIdType.MESH
F32 = jnp.float32
BF16 = jnp.bfloat16
NT = (((1,), (1,)), ((), ()))


def split(value):
    high = value.astype(BF16)
    return high, (value - high.astype(F32)).astype(BF16)


def dot(left, right, dims=None):
    if dims is None:
        return jnp.dot(left, right, preferred_element_type=F32)
    return lax.dot_general(left, right, dims, preferred_element_type=F32)


def fold(chunk):
    rows, cols = chunk.shape
    summed = jnp.sum(chunk.reshape(rows // 8, 8, cols), axis=0)
    total = summed[:, :LANES]
    for first in range(LANES, cols, LANES):
        total = total + summed[:, first : first + LANES]
    return total


def kernel(
    sizes,
    kappa_hbm,
    tau_hbm,
    value_hbm,
    weight_hbm,
    cell_hbm,
    blocks_ref,
    field_ref,
    fit_ref,
    start_buf,
    image_buf,
    stiff_buf,
    couple_buf,
    second_buf,
    observed_buf,
    row_hot,
    lon_hot,
    slot_hot,
    station_out,
    station_in,
    back_out,
    back_in,
    edge_out,
    edge_in,
    pair_in,
    level_out,
    level_in,
    columns,
    kappa_ref,
    tau_ref,
    value_ref,
    weight_ref,
    cell_ref,
    sum_out,
    sum_in,
    station_send,
    station_recv,
    back_send,
    back_recv,
    edge_send,
    edge_recv,
    pair_send,
    pair_recv,
    level_send,
    level_recv,
    load_sem,
    plane_send,
    plane_recv,
    sum_send,
    sum_recv,
):
    n_lon, n_lat, n_tm, hours, lats, lons, stations, padded = sizes
    owners = n_lat * n_tm
    capacity = stations // owners
    slots = owners * padded
    members = n_lon * owners
    lon, lat, tm = lax.axis_index("lon"), lax.axis_index("lat"), lax.axis_index("tm")
    owner = lat * n_tm + tm
    member = lon * owners + owner
    edge_hour = jnp.where(tm == 0, hours - 1, 0)
    chunks = range(0, lats, ROWS)

    def place(index):
        return {
            "lon": lax.div(index, owners),
            "lat": lax.rem(lax.div(index, n_tm), n_lat),
            "tm": lax.rem(index, n_tm),
        }

    def place_owner(index):
        return {"lon": lon, "lat": lax.div(index, n_tm), "tm": lax.rem(index, n_tm)}

    loads = [
        pltpu.make_async_copy(source, target, load_sem.at[index])
        for index, (source, target) in enumerate(
            [
                (value_hbm, value_ref),
                (weight_hbm, weight_ref),
                (cell_hbm, cell_ref),
                (kappa_hbm, kappa_ref),
                (tau_hbm, tau_ref),
            ]
        )
    ]
    for load in loads:
        load.start()
    barrier = pltpu.get_barrier_semaphore()

    def greet(step, carry):
        pl.semaphore_signal(
            barrier, inc=1, device_id=place(lax.rem(member + step, members)), device_id_type=MESH
        )
        return carry

    lax.fori_loop(1, members, greet, 0)

    for load in loads:
        load.wait()
    zeros = jnp.zeros((6, lats), F32)
    coefficients = (kappa_ref, tau_ref)
    sides = jnp.concatenate(
        [ref[:, lons - 1 : lons] for ref in coefficients]
        + [ref[:, 0:1] for ref in coefficients]
        + [jnp.zeros((lats, LANES - 4), F32)],
        axis=1,
    ).T
    level_out[0] = jnp.concatenate([sides[0:2], zeros], axis=0)
    level_out[1] = jnp.concatenate([sides[2:4], zeros], axis=0)
    zeros = jnp.zeros((6, lons), F32)
    level_out[2] = jnp.concatenate([ref[lats - 1 : lats, :] for ref in coefficients] + [zeros], axis=0)
    level_out[3] = jnp.concatenate([ref[0:1, :] for ref in coefficients] + [zeros], axis=0)
    for ref in (start_buf, image_buf):
        for hour in range(hours):
            ref[hour, 0:PAD, :] = jnp.zeros((PAD, lons), F32)
            ref[hour, PAD + lats :, :] = jnp.zeros((PAD, lons), F32)

    live = lax.broadcasted_iota(jnp.int32, (1, stations), 1) < blocks_ref[0] * BLOCK
    weight = jnp.where(live, weight_ref[...], 0.0)
    lon_at, lat_at, hour_at = cell_ref[0:1, :], cell_ref[1:2, :], cell_ref[2:3, :]
    own_lat = jnp.zeros_like(lat_at)
    for band in range(1, n_lat):
        own_lat = own_lat + (lat_at >= band * lats).astype(jnp.int32)
    own_tm = jnp.zeros_like(lat_at)
    for group in range(1, n_tm):
        own_tm = own_tm + (hour_at >= group * hours).astype(jnp.int32)
    away = own_lat * n_tm + own_tm - owner
    away = jnp.where(away < 0, away + owners, away)
    row_at = (hour_at - own_tm * hours) * lats + lat_at - own_lat * lats
    col_at = lon_at - lon * lons
    kinds = max(16, owners)
    hot = lax.broadcasted_iota(jnp.int32, (kinds, stations), 0) == away
    earlier = lax.broadcasted_iota(jnp.int32, (stations, stations), 0) < lax.broadcasted_iota(
        jnp.int32, (stations, stations), 1
    )
    counts = dot(hot.astype(F32).astype(BF16), earlier.astype(F32).astype(BF16))
    rank = jnp.sum(jnp.where(hot, counts, 0.0), axis=0, keepdims=True).astype(jnp.int32)
    slot = away * padded + rank
    slot_hot[...] = (
        (lax.broadcasted_iota(jnp.int32, (slots, stations), 0) == slot).astype(F32).astype(BF16)
    )
    payload = jnp.concatenate(
        [
            weight,
            weight * value_ref[...],
            row_at.astype(F32),
            col_at.astype(F32),
            jnp.zeros((4, stations), F32),
        ],
        axis=0,
    )
    high, low = split(payload)
    both = dot(jnp.concatenate([high, low], axis=0), slot_hot[...], NT)
    packed = both[:8] + both[8:]
    for step in range(owners):
        chunk = packed[:, step * padded : (step + 1) * padded]
        if step == 0:
            station_in[owners - 1] = chunk
        else:
            station_out[step - 1] = chunk

    lane = lax.broadcasted_iota(jnp.int32, (ROWS, lons), 1)
    lon_up, lon_down = lax.rem(lon + 1, n_lon), lax.rem(lon + n_lon - 1, n_lon)
    lat_up, lat_down = lax.rem(lat + 1, n_lat), lax.rem(lat + n_lat - 1, n_lat)
    pair = lax.rem(tm + 1, n_tm)
    ways = (0, 1, 2, 4, 5) if n_lat == 2 else tuple(range(8))
    slot_of = (0, 1, 2, 2, 4, 5, 4, 5) if n_lat == 2 else tuple(range(8))
    upward = jnp.where(lat == 0, 2, 3) if n_lat == 2 else 2
    targets = (
        (0, lon_up, lat),
        (1, lon_down, lat),
        (upward, lon, lat_up),
        (3, lon, lat_down),
        (upward, lon_up, lat_up),
        (upward, lon_down, lat_up),
        (3, lon_up, lat_down),
        (3, lon_down, lat_down),
    )

    def level_copies():
        copies = []
        for way in ways:
            if way < 4:
                tile, to_lon, to_lat = targets[way]
                copies.append(
                    pltpu.make_async_remote_copy(
                        src_ref=level_out.at[tile],
                        dst_ref=level_in.at[way],
                        send_sem=level_send.at[way],
                        recv_sem=level_recv.at[way],
                        device_id={"lon": to_lon, "lat": to_lat, "tm": tm},
                        device_id_type=MESH,
                    )
                )
        return copies

    pl.semaphore_wait(barrier, members - 1)

    def station_copy(step):
        return pltpu.make_async_remote_copy(
            src_ref=station_out.at[step - 1],
            dst_ref=station_in.at[step - 1],
            send_sem=station_send.at[step - 1],
            recv_sem=station_recv.at[step - 1],
            device_id=place_owner(lax.rem(owner + step, owners)),
            device_id_type=MESH,
        )

    for step in range(1, owners):
        station_copy(step).start()
    for copy in level_copies():
        copy.start()
    for step in range(1, owners):
        station_copy(step).wait()

    arrived = jnp.concatenate([station_in[index] for index in range(owners)], axis=1)
    here_row = arrived[2:3].astype(jnp.int32)
    here_col = arrived[3:4].astype(jnp.int32)
    cells = hours * lats
    row_hot[...] = (
        (lax.broadcasted_iota(jnp.int32, (cells, slots), 0) == here_row).astype(F32).astype(BF16)
    )
    col_mask = lax.broadcasted_iota(jnp.int32, (lons, slots), 0) == here_col
    lon_hot[...] = col_mask.astype(F32).astype(BF16)

    def spread(quantity):
        high, low = split(jnp.where(col_mask, quantity, 0.0))
        return high, low

    weight_high, weight_low = spread(arrived[0:1])
    right_high, right_low = spread(arrived[1:2])

    for hour in range(hours):
        hot_rows = row_hot[hour * lats : (hour + 1) * lats, :]
        start_buf[hour, PAD : PAD + lats, :] = dot(hot_rows, right_high, NT) + dot(
            hot_rows, right_low, NT
        )

    def edge_copies(phase):
        copies = []
        for across in range(2):
            for way in ways:
                tile, to_lon, to_lat = targets[way]
                index = across * 8 + way
                copies.append(
                    pltpu.make_async_remote_copy(
                        src_ref=edge_out.at[phase, tile],
                        dst_ref=edge_in.at[phase, index],
                        send_sem=edge_send.at[phase, index],
                        recv_sem=edge_recv.at[phase, index],
                        device_id={"lon": to_lon, "lat": to_lat, "tm": pair if across else tm},
                        device_id_type=MESH,
                    )
                )
        copies.append(
            pltpu.make_async_remote_copy(
                src_ref=edge_out.at[phase],
                dst_ref=pair_in.at[phase],
                send_sem=pair_send.at[phase],
                recv_sem=pair_recv.at[phase],
                device_id={"lon": lon, "lat": lat, "tm": pair},
                device_id_type=MESH,
            )
        )
        return copies

    def plane_copy(ref, which):
        return pltpu.make_async_remote_copy(
            src_ref=ref.at[edge_hour, pl.ds(PAD, lats)],
            dst_ref=ref.at[hours, pl.ds(PAD, lats)],
            send_sem=plane_send.at[which],
            recv_sem=plane_recv.at[which],
            device_id={"lon": lon, "lat": lat, "tm": pair},
            device_id_type=MESH,
        )

    def send_edges(ref, phase):
        beside = [
            ref[hour, PAD : PAD + lats, at : at + 1]
            for at in (lons - 2, lons - 1, 0, 1)
            for hour in range(hours)
        ]
        turned = jnp.concatenate(
            beside + [jnp.zeros((lats, LANES - 4 * hours), F32)], axis=1
        ).T
        edge_out[phase, 0] = turned[: 2 * hours]
        edge_out[phase, 1] = turned[2 * hours : 4 * hours]
        for tile, first in ((2, lats - 2), (3, 0)):
            edge_out[phase, tile] = jnp.concatenate(
                [
                    ref[hour, PAD + at : PAD + at + 1, :]
                    for at in (first, first + 1)
                    for hour in range(hours)
                ],
                axis=0,
            )
        for copy in edge_copies(phase):
            copy.start()

    def timeline(own, other, second):
        at = second * hours
        foreign = jnp.where(tm == 0, other[at : at + 1], other[at + hours - 1 : at + hours])
        return jnp.concatenate(
            [
                jnp.where(tm == 0, 0.0, foreign),
                own[at : at + hours],
                jnp.where(tm == 0, foreign, 0.0),
                jnp.zeros((8 - hours - 2, own.shape[1]), F32),
            ],
            axis=0,
        )

    hour_line = lax.broadcasted_iota(jnp.int32, (8, 1), 0)
    at_edge = (hour_line == 1) & (tm == 0) | (hour_line == hours) & (tm == n_tm - 1)

    def outer(far, near, inside, low, high, kappa, tau):
        length = near.shape[1]
        along = lax.broadcasted_iota(jnp.int32, (8, length), 1)
        beside = (
            far
            + inside
            + jnp.where(along == 0, low, pltpu.roll(near, 1, 1))
            + jnp.where(along == length - 1, high, pltpu.roll(near, length - 1, 1))
        )
        stiff = (kappa + 1.0) * near - 0.25 * beside
        diagonal = jnp.where(at_edge, 1.0, 1.0 + tau * tau)
        return diagonal * stiff - tau * (pltpu.roll(stiff, 1, 0) + pltpu.roll(stiff, 7, 0))

    def take_edges(ref, phase):
        for copy in edge_copies(phase):
            copy.wait()
        own = [edge_in[phase, slot_of[way]] for way in range(8)]
        other = [edge_in[phase, 8 + slot_of[way]] for way in range(8)]
        lines = {}
        for way in range(8):
            from_below = way in (0, 2, 4, 5)
            lines[way] = timeline(own[way], other[way], 1 if from_below else 0)
            if way < 4:
                lines[way, "far"] = timeline(own[way], other[way], 0 if from_below else 1)
        for way in (2, 4, 5):
            lines[way] = jnp.where(lat == 0, 0.0, lines[way])
        for way in (3, 6, 7):
            lines[way] = jnp.where(lat == n_lat - 1, 0.0, lines[way])
        within = [
            timeline(edge_out[phase, tile], pair_in[phase, tile], second)
            for tile, second in ((1, 0), (0, 1), (3, 0), (2, 1))
        ]
        corner = {
            way: lines[way][:, lons - 1 : lons] if way in (4, 6) else lines[way][:, 0:1]
            for way in (4, 5, 6, 7)
        }
        ends = {0: (4, 6), 1: (5, 7), 2: (4, 5), 3: (6, 7)}
        coupled = []
        for way in range(4):
            level = level_in[slot_of[way]]
            low, high = ends[way]
            coupled.append(
                outer(
                    lines[way, "far"],
                    lines[way],
                    within[way],
                    corner[low],
                    corner[high],
                    level[0:1],
                    level[1:2],
                )
            )
        coupled[2] = jnp.where(lat == 0, 0.0, coupled[2])
        coupled[3] = jnp.where(lat == n_lat - 1, 0.0, coupled[3])
        foreign = [
            jnp.where(tm == 0, lines[way][hours + 1 : hours + 2], lines[way][0:1])
            for way in range(4)
        ]
        columns[...] = jnp.concatenate(
            [
                lines[0][1 : hours + 1],
                foreign[0],
                jnp.zeros((7 - hours, lats), F32),
                lines[1][1 : hours + 1],
                foreign[1],
                jnp.zeros((7 - hours, lats), F32),
                coupled[0][1 : hours + 1],
                coupled[1][1 : hours + 1],
                jnp.zeros((LANES - 16 - 2 * hours, lats), F32),
            ],
            axis=0,
        ).T
        ref[hours, PAD - 1 : PAD, :] = foreign[2]
        ref[hours, PAD + lats : PAD + lats + 1, :] = foreign[3]
        for hour in range(hours):
            at = slice(hour + 1, hour + 2)
            stiff_buf[hour, 0:1, :] = stiff_buf[hour, 0:1, :] - 0.25 * lines[2][at]
            stiff_buf[hour, lats - 1 : lats, :] = (
                stiff_buf[hour, lats - 1 : lats, :] - 0.25 * lines[3][at]
            )
            couple_buf[hour, PAD - 1 : PAD, :] = coupled[2][at]
            couple_buf[hour, PAD + lats : PAD + lats + 1, :] = coupled[3][at]

    def stiffen(ref, hour, row, left=None, right=None):
        centre = ref[hour, PAD + row : PAD + row + ROWS, :]
        rows = slice(row, row + ROWS)
        if left is None:
            left, right = 0.0, 0.0
        else:
            left, right = columns[rows, left : left + 1], columns[rows, right : right + 1]
        beside = (
            jnp.where(lane == 0, left, pltpu.roll(centre, 1, 1))
            + jnp.where(lane == lons - 1, right, pltpu.roll(centre, lons - 1, 1))
            + ref[hour, PAD + row - 1 : PAD + row - 1 + ROWS, :]
            + ref[hour, PAD + row + 1 : PAD + row + 1 + ROWS, :]
        )
        return (kappa_ref[rows, :] + 1.0) * centre - 0.25 * beside

    def couple(row):
        rows = slice(row, row + ROWS)
        tau = tau_ref[rows, :]
        inner = 1.0 + tau * tau
        plane = []
        for hour in range(hours):
            beside = jnp.where(
                lane == 0,
                columns[rows, hour : hour + 1],
                jnp.where(lane == lons - 1, columns[rows, 8 + hour : 9 + hour], 0.0),
            )
            plane.append(stiff_buf[hour, rows, :] - 0.25 * beside)
        plane.append(stiff_buf[hours, rows, :])
        for hour in range(hours):
            diagonal = inner
            if hour == 0:
                below = jnp.where(tm == 0, 0.0, plane[hours])
                diagonal = jnp.where(tm == 0, 1.0, inner)
            else:
                below = plane[hour - 1]
            if hour == hours - 1:
                above = jnp.where(tm == n_tm - 1, 0.0, plane[hours])
                diagonal = jnp.where(tm == n_tm - 1, 1.0, inner)
            else:
                above = plane[hour + 1]
            couple_buf[hour, PAD + row : PAD + row + ROWS, :] = diagonal * plane[hour] - tau * (
                below + above
            )

    def sum_start(which, partial):
        sum_out[which] = jnp.sum(partial, axis=0, keepdims=True)

        def send(step, carry):
            pltpu.make_async_remote_copy(
                src_ref=sum_out.at[which],
                dst_ref=sum_in.at[which, step - 1],
                send_sem=sum_send.at[which],
                recv_sem=sum_recv.at[which],
                device_id=place(lax.rem(member + step, members)),
                device_id_type=MESH,
            ).start()
            return carry

        if members <= 16:
            for step in range(1, members):
                send(step, 0)
        else:
            lax.fori_loop(1, members, send, 0)

    def sum_finish(which):
        pltpu.make_async_remote_copy(
            src_ref=sum_in.at[which],
            dst_ref=sum_in.at[which],
            send_sem=sum_send.at[which],
            recv_sem=sum_recv.at[which],
            device_id=place(lax.rem(member + 1, members)),
            device_id_type=MESH,
        ).wait()
        total = jnp.sum(sum_in[which], axis=0) + sum_out[which]
        return jnp.sum(total, axis=1, keepdims=True)

    def gather(ref):
        picked = jnp.zeros((1, slots), F32)
        for hour in range(hours):
            high, low = split(ref[hour, PAD : PAD + lats, :])
            found = dot(high, lon_hot[...]) + dot(low, lon_hot[...])
            hot_rows = row_hot[hour * lats : (hour + 1) * lats, :].astype(F32)
            picked = picked + jnp.sum(found * hot_rows, axis=0, keepdims=True)
        return picked

    plane_copy(start_buf, 0).start()
    send_edges(start_buf, 0)
    for hour in range(hours):
        hot_rows = row_hot[hour * lats : (hour + 1) * lats, :]
        observed_buf[hour] = dot(hot_rows, weight_high, NT) + dot(hot_rows, weight_low, NT)
    norm_part = jnp.zeros((8, LANES), F32)
    for hour in range(hours):
        for row in chunks:
            chunk = start_buf[hour, PAD + row : PAD + row + ROWS, :]
            norm_part = norm_part + fold(chunk * chunk)
    sum_start(0, norm_part)

    def image(source, target, base, phase, meanwhile):
        for hour in range(hours):
            for row in chunks:
                stiff_buf[hour, row : row + ROWS, :] = stiffen(source, hour, row)
        kept = meanwhile()
        plane_copy(source, phase).wait()
        take_edges(source, phase)
        for row in chunks:
            stiff_buf[hours, row : row + ROWS, :] = stiffen(source, hours, row, hours, 8 + hours)
        for row in chunks:
            couple(row)
        part = jnp.zeros((8, LANES), F32)
        for hour in range(hours):
            for row in chunks:
                at = slice(base + row, base + row + ROWS)
                own = source[hour, PAD + row : PAD + row + ROWS, :]
                result = (
                    stiffen(couple_buf, hour, row, 16 + hour, 16 + hours + hour)
                    + observed_buf[hour, row : row + ROWS, :] * own
                )
                target[hour, at, :] = result
                if phase == 0:
                    part = part + fold(own * result)
        return part, kept

    def first_meanwhile():
        picked = gather(start_buf)
        for copy in level_copies():
            copy.wait()
        return picked

    part, picked_start = image(start_buf, image_buf, PAD, 0, first_meanwhile)
    plane_copy(image_buf, 1).start()
    send_edges(image_buf, 1)
    sum_start(1, part)
    image(image_buf, second_buf, 0, 1, lambda: None)

    norm = sum_finish(0)
    step_first = norm / sum_finish(1)
    part = jnp.zeros((8, LANES), F32)
    for hour in range(hours):
        for row in chunks:
            at = slice(PAD + row, PAD + row + ROWS)
            rest = start_buf[hour, at, :] - step_first * image_buf[hour, at, :]
            couple_buf[hour, at, :] = rest
            part = part + fold(rest * rest)
    sum_start(2, part)
    ratio = sum_finish(2)
    norm_next = ratio
    ratio = ratio / norm
    part = jnp.zeros((8, LANES), F32)
    for hour in range(hours):
        for row in chunks:
            at = slice(PAD + row, PAD + row + ROWS)
            applied = image_buf[hour, at, :]
            direction = couple_buf[hour, at, :] + ratio * start_buf[hour, at, :]
            turned = (
                applied - step_first * second_buf[hour, row : row + ROWS, :] + ratio * applied
            )
            couple_buf[hour, at, :] = direction
            part = part + fold(direction * turned)
    sum_start(3, part)

    picked = jnp.concatenate(
        [picked_start, gather(couple_buf), jnp.zeros((6, slots), F32)], axis=0
    )
    for step in range(1, owners + 1):
        chunk = picked[:, (step - 1) * padded : step * padded]
        if step == owners:
            back_in[0] = chunk
        else:
            back_out[step - 1] = chunk

    def back_copy(step):
        return pltpu.make_async_remote_copy(
            src_ref=back_out.at[step - 1],
            dst_ref=back_in.at[step],
            send_sem=back_send.at[step - 1],
            recv_sem=back_recv.at[step - 1],
            device_id=place_owner(lax.rem(owner + owners - step, owners)),
            device_id_type=MESH,
        )

    for step in range(1, owners):
        back_copy(step).start()
    for step in range(1, owners):
        back_copy(step).wait()
    returned = jnp.concatenate([back_in[index] for index in range(owners)], axis=1)
    high, low = split(returned)
    both = dot(jnp.concatenate([high, low], axis=0), slot_hot[...])
    fitted = both[:8] + both[8:]

    step_second = norm_next / sum_finish(3)
    for hour in range(hours):
        for row in chunks:
            at = slice(PAD + row, PAD + row + ROWS)
            field_ref[hour, row : row + ROWS, :] = (
                step_first * start_buf[hour, at, :] + step_second * couple_buf[hour, at, :]
            )
    fit_ref[...] = jnp.where(live, step_first * fitted[0:1] + step_second * fitted[1:2], 0.0)


def body(kappa_squared, time_coupling, station_value, station_weight, station_cell, slab_blocks):
    n_lon, n_lat, n_tm = (lax.axis_size(axis) for axis in ("lon", "lat", "tm"))
    lats, lons = kappa_squared.shape
    stations = station_value.shape[0]
    hours = HOURS // n_tm
    owners = n_lat * n_tm
    members = n_lon * owners
    padded = -(-(stations // owners) // LANES) * LANES
    slots = owners * padded
    sizes = (n_lon, n_lat, n_tm, hours, lats, lons, stations, padded)
    tall = lats + 2 * PAD
    vmem = pl.BlockSpec(memory_space=pltpu.VMEM)
    dma = pltpu.SemaphoreType.DMA
    field, fit = pl.pallas_call(
        functools.partial(kernel, sizes),
        out_shape=(
            jax.ShapeDtypeStruct((hours, lats, lons), F32),
            jax.ShapeDtypeStruct((1, stations), F32),
        ),
        in_specs=[pl.BlockSpec(memory_space=pl.ANY)] * 5 + [pl.BlockSpec(memory_space=pltpu.SMEM)],
        out_specs=(vmem, vmem),
        scratch_shapes=[
            pltpu.VMEM((hours + 1, tall, lons), F32),
            pltpu.VMEM((hours + 1, tall, lons), F32),
            pltpu.VMEM((hours + 1, lats, lons), F32),
            pltpu.VMEM((hours, tall, lons), F32),
            pltpu.VMEM((hours, lats, lons), F32),
            pltpu.VMEM((hours, lats, lons), F32),
            pltpu.VMEM((hours * lats, slots), BF16),
            pltpu.VMEM((lons, slots), BF16),
            pltpu.VMEM((slots, stations), BF16),
            pltpu.VMEM((owners - 1, 8, padded), F32),
            pltpu.VMEM((owners, 8, padded), F32),
            pltpu.VMEM((owners - 1, 8, padded), F32),
            pltpu.VMEM((owners, 8, padded), F32),
            pltpu.VMEM((2, 4, 2 * hours, lats), F32),
            pltpu.VMEM((2, 16, 2 * hours, lats), F32),
            pltpu.VMEM((2, 4, 2 * hours, lats), F32),
            pltpu.VMEM((4, 8, lats), F32),
            pltpu.VMEM((4, 8, lats), F32),
            pltpu.VMEM((lats, LANES), F32),
            pltpu.VMEM((lats, lons), F32),
            pltpu.VMEM((lats, lons), F32),
            pltpu.VMEM((1, stations), F32),
            pltpu.VMEM((1, stations), F32),
            pltpu.VMEM((3, stations), jnp.int32),
            pltpu.VMEM((4, 1, LANES), F32),
            pltpu.VMEM((4, members - 1, 1, LANES), F32),
            dma((owners - 1,)),
            dma((owners - 1,)),
            dma((owners - 1,)),
            dma((owners - 1,)),
            dma((2, 16)),
            dma((2, 16)),
            dma((2,)),
            dma((2,)),
            dma((4,)),
            dma((4,)),
            dma((5,)),
            dma((2,)),
            dma((2,)),
            dma((4,)),
            dma((4,)),
        ],
        compiler_params=pltpu.CompilerParams(
            collective_id=0, has_side_effects=True, vmem_limit_bytes=48 * 1024 * 1024
        ),
    )(
        kappa_squared,
        time_coupling,
        station_value.reshape(1, stations),
        station_weight.reshape(1, stations),
        station_cell,
        slab_blocks,
    )
    return field, fit.reshape(stations)


def solution(mesh):
    rows = P(("groups", "lon", "lat", "tm"))
    return jax.shard_map(
        body,
        mesh=mesh,
        in_specs=(
            P("lat", "lon"),
            P("lat", "lon"),
            rows,
            rows,
            P(None, ("groups", "lon", "lat", "tm")),
            P(("groups", "lon")),
        ),
        out_specs=(P(("groups", "tm"), "lat", "lon"), rows),
        check_vma=False,
    )
```

```python
import functools

import jax
import jax.numpy as jnp
from jax import lax
from jax.experimental import pallas as pl
from jax.experimental.pallas import tpu as pltpu
from jax.sharding import PartitionSpec as P

HOURS = 8
BLOCK = 128
PAD = 8
ROWS = 64
LANES = 128
VMEM_LIMIT = 62 * 1024 * 1024
MESH = pl.DeviceIdType.MESH
F32 = jnp.float32
BF16 = jnp.bfloat16
NT = (((1,), (1,)), ((), ()))


def split(value):
    high = value.astype(BF16)
    return high, (value - high.astype(F32)).astype(BF16)


def dot(left, right, dims=None):
    if dims is None:
        return jnp.dot(left, right, preferred_element_type=F32)
    return lax.dot_general(left, right, dims, preferred_element_type=F32)


def fold(chunk):
    rows, cols = chunk.shape
    summed = jnp.sum(chunk.reshape(rows // 8, 8, cols), axis=0)
    total = summed[:, :LANES]
    for first in range(LANES, cols, LANES):
        total = total + summed[:, first : first + LANES]
    return total


def kernel(
    sizes,
    kappa_hbm,
    tau_hbm,
    value_hbm,
    weight_hbm,
    cell_hbm,
    blocks_ref,
    field_ref,
    fit_ref,
    start_buf,
    image_buf,
    stiff_buf,
    couple_buf,
    second_buf,
    observed_buf,
    row_hot,
    lon_hot,
    slot_hot,
    station_out,
    station_in,
    back_out,
    back_in,
    edge_out,
    edge_in,
    pair_in,
    level_out,
    level_in,
    columns,
    kappa_ref,
    tau_ref,
    value_ref,
    weight_ref,
    cell_ref,
    sum_out,
    sum_in,
    station_send,
    station_recv,
    back_send,
    back_recv,
    edge_send,
    edge_recv,
    pair_send,
    pair_recv,
    level_send,
    level_recv,
    load_sem,
    plane_send,
    plane_recv,
    sum_send,
    sum_recv,
):
    n_lon, n_lat, n_tm, hours, lats, lons, stations, padded = sizes
    owners = n_lat * n_tm
    capacity = stations // owners
    slots = owners * padded
    members = n_lon * owners
    lon, lat, tm = lax.axis_index("lon"), lax.axis_index("lat"), lax.axis_index("tm")
    owner = lat * n_tm + tm
    edge_hour = jnp.where(tm == 0, hours - 1, 0)
    chunks = range(0, lats, ROWS)

    def others(act):
        def at_lon(step_lon, skip):
            to_lon = lon + step_lon
            to_lon = jnp.where(to_lon >= n_lon, to_lon - n_lon, to_lon)
            for step_lat in range(n_lat):
                to_lat = lat + step_lat
                to_lat = jnp.where(to_lat >= n_lat, to_lat - n_lat, to_lat)
                for step_tm in range(n_tm):
                    if skip and step_lat == 0 and step_tm == 0:
                        continue
                    to_tm = tm + step_tm
                    to_tm = jnp.where(to_tm >= n_tm, to_tm - n_tm, to_tm)
                    slot = (step_lon * n_lat + step_lat) * n_tm + step_tm - 1
                    act({"lon": to_lon, "lat": to_lat, "tm": to_tm}, slot)

        at_lon(0, True)
        if n_lon <= 4:
            for step_lon in range(1, n_lon):
                at_lon(step_lon, False)
        else:
            lax.fori_loop(1, n_lon, lambda step, carry: (at_lon(step, False), carry)[1], 0)

    def place_owner(index):
        return {"lon": lon, "lat": lax.div(index, n_tm), "tm": lax.rem(index, n_tm)}

    loads = [
        pltpu.make_async_copy(source, target, load_sem.at[index])
        for index, (source, target) in enumerate(
            [
                (value_hbm, value_ref),
                (weight_hbm, weight_ref),
                (cell_hbm, cell_ref),
                (kappa_hbm, kappa_ref),
                (tau_hbm, tau_ref),
            ]
        )
    ]
    for load in loads:
        load.start()
    barrier = pltpu.get_barrier_semaphore()

    def greet(place, slot):
        pl.semaphore_signal(barrier, inc=1, device_id=place, device_id_type=MESH)

    others(greet)

    for load in loads:
        load.wait()
    zeros = jnp.zeros((6, lats), F32)
    coefficients = (kappa_ref, tau_ref)
    sides = jnp.concatenate(
        [ref[:, lons - 1 : lons] for ref in coefficients]
        + [ref[:, 0:1] for ref in coefficients]
        + [jnp.zeros((lats, LANES - 4), F32)],
        axis=1,
    ).T
    level_out[0] = jnp.concatenate([sides[0:2], zeros], axis=0)
    level_out[1] = jnp.concatenate([sides[2:4], zeros], axis=0)
    zeros = jnp.zeros((6, lons), F32)
    level_out[2] = jnp.concatenate([ref[lats - 1 : lats, :] for ref in coefficients] + [zeros], axis=0)
    level_out[3] = jnp.concatenate([ref[0:1, :] for ref in coefficients] + [zeros], axis=0)
    for ref in (start_buf, image_buf):
        for hour in range(hours):
            ref[hour, 0:PAD, :] = jnp.zeros((PAD, lons), F32)
            ref[hour, PAD + lats :, :] = jnp.zeros((PAD, lons), F32)

    live = lax.broadcasted_iota(jnp.int32, (1, stations), 1) < blocks_ref[0] * BLOCK
    weight = jnp.where(live, weight_ref[...], 0.0)
    lon_at, lat_at, hour_at = cell_ref[0:1, :], cell_ref[1:2, :], cell_ref[2:3, :]
    own_lat = jnp.zeros_like(lat_at)
    for band in range(1, n_lat):
        own_lat = own_lat + (lat_at >= band * lats).astype(jnp.int32)
    own_tm = jnp.zeros_like(lat_at)
    for group in range(1, n_tm):
        own_tm = own_tm + (hour_at >= group * hours).astype(jnp.int32)
    away = own_lat * n_tm + own_tm - owner
    away = jnp.where(away < 0, away + owners, away)
    row_at = (hour_at - own_tm * hours) * lats + lat_at - own_lat * lats
    col_at = lon_at - lon * lons
    kinds = max(16, owners)
    hot = lax.broadcasted_iota(jnp.int32, (kinds, stations), 0) == away
    earlier = lax.broadcasted_iota(jnp.int32, (stations, stations), 0) < lax.broadcasted_iota(
        jnp.int32, (stations, stations), 1
    )
    counts = dot(hot.astype(F32).astype(BF16), earlier.astype(F32).astype(BF16))
    rank = jnp.sum(jnp.where(hot, counts, 0.0), axis=0, keepdims=True).astype(jnp.int32)
    slot = away * padded + rank
    slot_hot[...] = (
        (lax.broadcasted_iota(jnp.int32, (slots, stations), 0) == slot).astype(F32).astype(BF16)
    )
    payload = jnp.concatenate(
        [
            weight,
            weight * value_ref[...],
            row_at.astype(F32),
            col_at.astype(F32),
            jnp.zeros((4, stations), F32),
        ],
        axis=0,
    )
    high, low = split(payload)
    both = dot(jnp.concatenate([high, low], axis=0), slot_hot[...], NT)
    packed = both[:8] + both[8:]
    for step in range(owners):
        chunk = packed[:, step * padded : (step + 1) * padded]
        if step == 0:
            station_in[owners - 1] = chunk
        else:
            station_out[step - 1] = chunk

    lane = lax.broadcasted_iota(jnp.int32, (ROWS, lons), 1)
    lon_up, lon_down = lax.rem(lon + 1, n_lon), lax.rem(lon + n_lon - 1, n_lon)
    lat_up, lat_down = lax.rem(lat + 1, n_lat), lax.rem(lat + n_lat - 1, n_lat)
    pair = lax.rem(tm + 1, n_tm)
    ways = (0, 1, 2, 4, 5) if n_lat == 2 else tuple(range(8))
    slot_of = (0, 1, 2, 2, 4, 5, 4, 5) if n_lat == 2 else tuple(range(8))
    upward = jnp.where(lat == 0, 2, 3) if n_lat == 2 else 2
    targets = (
        (0, lon_up, lat),
        (1, lon_down, lat),
        (upward, lon, lat_up),
        (3, lon, lat_down),
        (upward, lon_up, lat_up),
        (upward, lon_down, lat_up),
        (3, lon_up, lat_down),
        (3, lon_down, lat_down),
    )

    def level_copies():
        copies = []
        for way in ways:
            if way < 4:
                tile, to_lon, to_lat = targets[way]
                copies.append(
                    pltpu.make_async_remote_copy(
                        src_ref=level_out.at[tile],
                        dst_ref=level_in.at[way],
                        send_sem=level_send.at[way],
                        recv_sem=level_recv.at[way],
                        device_id={"lon": to_lon, "lat": to_lat, "tm": tm},
                        device_id_type=MESH,
                    )
                )
        return copies

    pl.semaphore_wait(barrier, members - 1)

    def station_copy(step):
        return pltpu.make_async_remote_copy(
            src_ref=station_out.at[step - 1],
            dst_ref=station_in.at[step - 1],
            send_sem=station_send.at[step - 1],
            recv_sem=station_recv.at[step - 1],
            device_id=place_owner(lax.rem(owner + step, owners)),
            device_id_type=MESH,
        )

    for step in range(1, owners):
        station_copy(step).start()
    for copy in level_copies():
        copy.start()
    for step in range(1, owners):
        station_copy(step).wait()

    arrived = jnp.concatenate([station_in[index] for index in range(owners)], axis=1)
    here_row = arrived[2:3].astype(jnp.int32)
    here_col = arrived[3:4].astype(jnp.int32)
    cells = hours * lats
    row_hot[...] = (
        (lax.broadcasted_iota(jnp.int32, (cells, slots), 0) == here_row).astype(F32).astype(BF16)
    )
    col_mask = lax.broadcasted_iota(jnp.int32, (lons, slots), 0) == here_col
    lon_hot[...] = col_mask.astype(F32).astype(BF16)

    def spread(quantity):
        high, low = split(jnp.where(col_mask, quantity, 0.0))
        return high, low

    weight_high, weight_low = spread(arrived[0:1])
    right_high, right_low = spread(arrived[1:2])

    for hour in range(hours):
        hot_rows = row_hot[hour * lats : (hour + 1) * lats, :]
        start_buf[hour, PAD : PAD + lats, :] = dot(hot_rows, right_high, NT) + dot(
            hot_rows, right_low, NT
        )

    def edge_copies(phase):
        copies = []
        for across in range(2):
            for way in ways:
                tile, to_lon, to_lat = targets[way]
                index = across * 8 + way
                source, target = edge_out.at[phase, tile], edge_in.at[phase, index]
                if way >= 4:
                    half = pl.ds(lons - LANES if way in (4, 6) else 0, LANES)
                    source, target = source.at[:, half], target.at[:, half]
                copies.append(
                    pltpu.make_async_remote_copy(
                        src_ref=source,
                        dst_ref=target,
                        send_sem=edge_send.at[phase, index],
                        recv_sem=edge_recv.at[phase, index],
                        device_id={"lon": to_lon, "lat": to_lat, "tm": pair if across else tm},
                        device_id_type=MESH,
                    )
                )
        copies.append(
            pltpu.make_async_remote_copy(
                src_ref=edge_out.at[phase],
                dst_ref=pair_in.at[phase],
                send_sem=pair_send.at[phase],
                recv_sem=pair_recv.at[phase],
                device_id={"lon": lon, "lat": lat, "tm": pair},
                device_id_type=MESH,
            )
        )
        return copies

    def plane_copy(ref, which):
        return pltpu.make_async_remote_copy(
            src_ref=ref.at[edge_hour, pl.ds(PAD, lats)],
            dst_ref=ref.at[hours, pl.ds(PAD, lats)],
            send_sem=plane_send.at[which],
            recv_sem=plane_recv.at[which],
            device_id={"lon": lon, "lat": lat, "tm": pair},
            device_id_type=MESH,
        )

    def send_edges(ref, phase):
        beside = [
            ref[hour, PAD : PAD + lats, at : at + 1]
            for at in (lons - 2, lons - 1, 0, 1)
            for hour in range(hours)
        ]
        turned = jnp.concatenate(
            beside + [jnp.zeros((lats, LANES - 4 * hours), F32)], axis=1
        ).T
        edge_out[phase, 0] = turned[: 2 * hours]
        edge_out[phase, 1] = turned[2 * hours : 4 * hours]
        for tile, first in ((2, lats - 2), (3, 0)):
            edge_out[phase, tile] = jnp.concatenate(
                [
                    ref[hour, PAD + at : PAD + at + 1, :]
                    for at in (first, first + 1)
                    for hour in range(hours)
                ],
                axis=0,
            )
        for copy in edge_copies(phase):
            copy.start()

    def timeline(own, other, second):
        at = second * hours
        foreign = jnp.where(tm == 0, other[at : at + 1], other[at + hours - 1 : at + hours])
        return jnp.concatenate(
            [
                jnp.where(tm == 0, 0.0, foreign),
                own[at : at + hours],
                jnp.where(tm == 0, foreign, 0.0),
                jnp.zeros((8 - hours - 2, own.shape[1]), F32),
            ],
            axis=0,
        )

    hour_line = lax.broadcasted_iota(jnp.int32, (8, 1), 0)
    at_edge = (hour_line == 1) & (tm == 0) | (hour_line == hours) & (tm == n_tm - 1)

    def outer(far, near, inside, low, high, kappa, tau):
        length = near.shape[1]
        along = lax.broadcasted_iota(jnp.int32, (8, length), 1)
        beside = (
            far
            + inside
            + jnp.where(along == 0, low, pltpu.roll(near, 1, 1))
            + jnp.where(along == length - 1, high, pltpu.roll(near, length - 1, 1))
        )
        stiff = (kappa + 1.0) * near - 0.25 * beside
        diagonal = jnp.where(at_edge, 1.0, 1.0 + tau * tau)
        return diagonal * stiff - tau * (pltpu.roll(stiff, 1, 0) + pltpu.roll(stiff, 7, 0))

    def take_edges(ref, phase):
        for copy in edge_copies(phase):
            copy.wait()
        span = {way: slice(lons - LANES, lons) for way in (4, 6)} | {
            way: slice(0, LANES) for way in (5, 7)
        }
        every = slice(0, lons)
        own = [edge_in[phase, slot_of[way], :, span.get(way, every)] for way in range(8)]
        other = [edge_in[phase, 8 + slot_of[way], :, span.get(way, every)] for way in range(8)]
        lines = {}
        for way in range(8):
            from_below = way in (0, 2, 4, 5)
            lines[way] = timeline(own[way], other[way], 1 if from_below else 0)
            if way < 4:
                lines[way, "far"] = timeline(own[way], other[way], 0 if from_below else 1)
        for way in (2, 4, 5):
            lines[way] = jnp.where(lat == 0, 0.0, lines[way])
        for way in (3, 6, 7):
            lines[way] = jnp.where(lat == n_lat - 1, 0.0, lines[way])
        within = [
            timeline(edge_out[phase, tile], pair_in[phase, tile], second)
            for tile, second in ((1, 0), (0, 1), (3, 0), (2, 1))
        ]
        corner = {
            way: lines[way][:, LANES - 1 :] if way in (4, 6) else lines[way][:, 0:1]
            for way in (4, 5, 6, 7)
        }
        ends = {0: (4, 6), 1: (5, 7), 2: (4, 5), 3: (6, 7)}
        coupled = []
        for way in range(4):
            level = level_in[slot_of[way]]
            low, high = ends[way]
            coupled.append(
                outer(
                    lines[way, "far"],
                    lines[way],
                    within[way],
                    corner[low],
                    corner[high],
                    level[0:1],
                    level[1:2],
                )
            )
        coupled[2] = jnp.where(lat == 0, 0.0, coupled[2])
        coupled[3] = jnp.where(lat == n_lat - 1, 0.0, coupled[3])
        foreign = [
            jnp.where(tm == 0, lines[way][hours + 1 : hours + 2], lines[way][0:1])
            for way in range(4)
        ]
        columns[...] = jnp.concatenate(
            [
                lines[0][1 : hours + 1],
                foreign[0],
                jnp.zeros((7 - hours, lats), F32),
                lines[1][1 : hours + 1],
                foreign[1],
                jnp.zeros((7 - hours, lats), F32),
                coupled[0][1 : hours + 1],
                coupled[1][1 : hours + 1],
                jnp.zeros((LANES - 16 - 2 * hours, lats), F32),
            ],
            axis=0,
        ).T
        ref[hours, PAD - 1 : PAD, :] = foreign[2]
        ref[hours, PAD + lats : PAD + lats + 1, :] = foreign[3]
        for hour in range(hours):
            at = slice(hour + 1, hour + 2)
            stiff_buf[hour, 0:1, :] = stiff_buf[hour, 0:1, :] - 0.25 * lines[2][at]
            stiff_buf[hour, lats - 1 : lats, :] = (
                stiff_buf[hour, lats - 1 : lats, :] - 0.25 * lines[3][at]
            )
            couple_buf[hour, PAD - 1 : PAD, :] = coupled[2][at]
            couple_buf[hour, PAD + lats : PAD + lats + 1, :] = coupled[3][at]

    def stiffen(ref, hour, row, left=None, right=None):
        centre = ref[hour, PAD + row : PAD + row + ROWS, :]
        rows = slice(row, row + ROWS)
        if left is None:
            left, right = 0.0, 0.0
        else:
            left, right = columns[rows, left : left + 1], columns[rows, right : right + 1]
        beside = (
            jnp.where(lane == 0, left, pltpu.roll(centre, 1, 1))
            + jnp.where(lane == lons - 1, right, pltpu.roll(centre, lons - 1, 1))
            + ref[hour, PAD + row - 1 : PAD + row - 1 + ROWS, :]
            + ref[hour, PAD + row + 1 : PAD + row + 1 + ROWS, :]
        )
        return (kappa_ref[rows, :] + 1.0) * centre - 0.25 * beside

    def couple(row):
        rows = slice(row, row + ROWS)
        tau = tau_ref[rows, :]
        inner = 1.0 + tau * tau
        plane = []
        for hour in range(hours):
            beside = jnp.where(
                lane == 0,
                columns[rows, hour : hour + 1],
                jnp.where(lane == lons - 1, columns[rows, 8 + hour : 9 + hour], 0.0),
            )
            plane.append(stiff_buf[hour, rows, :] - 0.25 * beside)
        plane.append(stiff_buf[hours, rows, :])
        for hour in range(hours):
            diagonal = inner
            if hour == 0:
                below = jnp.where(tm == 0, 0.0, plane[hours])
                diagonal = jnp.where(tm == 0, 1.0, inner)
            else:
                below = plane[hour - 1]
            if hour == hours - 1:
                above = jnp.where(tm == n_tm - 1, 0.0, plane[hours])
                diagonal = jnp.where(tm == n_tm - 1, 1.0, inner)
            else:
                above = plane[hour + 1]
            couple_buf[hour, PAD + row : PAD + row + ROWS, :] = diagonal * plane[hour] - tau * (
                below + above
            )

    def sum_start(which, partial):
        sum_out[which] = jnp.sum(partial, axis=0, keepdims=True)

        def send(place, slot):
            pltpu.make_async_remote_copy(
                src_ref=sum_out.at[which],
                dst_ref=sum_in.at[which, slot],
                send_sem=sum_send.at[which],
                recv_sem=sum_recv.at[which],
                device_id=place,
                device_id_type=MESH,
            ).start()

        others(send)

    def sum_finish(which):
        pltpu.make_async_remote_copy(
            src_ref=sum_in.at[which],
            dst_ref=sum_in.at[which],
            send_sem=sum_send.at[which],
            recv_sem=sum_recv.at[which],
            device_id={"lon": lon, "lat": lat, "tm": pair},
            device_id_type=MESH,
        ).wait()
        total = jnp.sum(sum_in[which], axis=0) + sum_out[which]
        return jnp.sum(total, axis=1, keepdims=True)

    def gather(ref):
        picked = jnp.zeros((1, slots), F32)
        for hour in range(hours):
            high, low = split(ref[hour, PAD : PAD + lats, :])
            found = dot(high, lon_hot[...]) + dot(low, lon_hot[...])
            hot_rows = row_hot[hour * lats : (hour + 1) * lats, :].astype(F32)
            picked = picked + jnp.sum(found * hot_rows, axis=0, keepdims=True)
        return picked

    plane_copy(start_buf, 0).start()
    send_edges(start_buf, 0)
    for hour in range(hours):
        hot_rows = row_hot[hour * lats : (hour + 1) * lats, :]
        observed_buf[hour] = dot(hot_rows, weight_high, NT) + dot(hot_rows, weight_low, NT)
    norm_part = jnp.zeros((8, LANES), F32)
    for hour in range(hours):
        for row in chunks:
            chunk = start_buf[hour, PAD + row : PAD + row + ROWS, :]
            norm_part = norm_part + fold(chunk * chunk)
    sum_start(0, norm_part)

    def image(source, target, base, phase, meanwhile):
        for hour in range(hours):
            for row in chunks:
                stiff_buf[hour, row : row + ROWS, :] = stiffen(source, hour, row)
        kept = meanwhile()
        plane_copy(source, phase).wait()
        take_edges(source, phase)
        for row in chunks:
            stiff_buf[hours, row : row + ROWS, :] = stiffen(source, hours, row, hours, 8 + hours)
        for row in chunks:
            couple(row)
        part = jnp.zeros((8, LANES), F32)
        for hour in range(hours):
            for row in chunks:
                at = slice(base + row, base + row + ROWS)
                own = source[hour, PAD + row : PAD + row + ROWS, :]
                result = (
                    stiffen(couple_buf, hour, row, 16 + hour, 16 + hours + hour)
                    + observed_buf[hour, row : row + ROWS, :] * own
                )
                target[hour, at, :] = result
                if phase == 0:
                    part = part + fold(own * result)
        return part, kept

    def first_meanwhile():
        picked = gather(start_buf)
        for copy in level_copies():
            copy.wait()
        return picked

    part, picked_start = image(start_buf, image_buf, PAD, 0, first_meanwhile)
    plane_copy(image_buf, 1).start()
    send_edges(image_buf, 1)
    sum_start(1, part)
    image(image_buf, second_buf, 0, 1, lambda: None)

    norm = sum_finish(0)
    step_first = norm / sum_finish(1)
    part = jnp.zeros((8, LANES), F32)
    for hour in range(hours):
        for row in chunks:
            at = slice(PAD + row, PAD + row + ROWS)
            rest = start_buf[hour, at, :] - step_first * image_buf[hour, at, :]
            couple_buf[hour, at, :] = rest
            part = part + fold(rest * rest)
    sum_start(2, part)

    picked = jnp.concatenate(
        [picked_start, gather(couple_buf), jnp.zeros((6, slots), F32)], axis=0
    )
    for step in range(1, owners + 1):
        chunk = picked[:, (step - 1) * padded : step * padded]
        if step == owners:
            back_in[0] = chunk
        else:
            back_out[step - 1] = chunk

    def back_copy(step):
        return pltpu.make_async_remote_copy(
            src_ref=back_out.at[step - 1],
            dst_ref=back_in.at[step],
            send_sem=back_send.at[step - 1],
            recv_sem=back_recv.at[step - 1],
            device_id=place_owner(lax.rem(owner + owners - step, owners)),
            device_id_type=MESH,
        )

    for step in range(1, owners):
        back_copy(step).start()
    for hour in range(hours):
        for row in chunks:
            at = slice(row, row + ROWS)
            second_buf[hour, at, :] = (
                image_buf[hour, PAD + row : PAD + row + ROWS, :]
                - step_first * second_buf[hour, at, :]
            )
    norm_next = sum_finish(2)
    ratio = norm_next / norm
    part = jnp.zeros((8, LANES), F32)
    for hour in range(hours):
        for row in chunks:
            at = slice(PAD + row, PAD + row + ROWS)
            direction = couple_buf[hour, at, :] + ratio * start_buf[hour, at, :]
            turned = second_buf[hour, row : row + ROWS, :] + ratio * image_buf[hour, at, :]
            couple_buf[hour, at, :] = direction
            part = part + fold(direction * turned)
    sum_start(3, part)

    for step in range(1, owners):
        back_copy(step).wait()
    returned = jnp.concatenate([back_in[index] for index in range(owners)], axis=1)
    high, low = split(returned)
    both = dot(jnp.concatenate([high, low], axis=0), slot_hot[...])
    fitted = both[:8] + both[8:]

    step_second = norm_next / sum_finish(3)
    for hour in range(hours):
        for row in chunks:
            at = slice(PAD + row, PAD + row + ROWS)
            field_ref[hour, row : row + ROWS, :] = (
                step_first * start_buf[hour, at, :] + step_second * couple_buf[hour, at, :]
            )
    fitted_at = step_first * fitted[0:1] + step_second * (fitted[1:2] + ratio * fitted[0:1])
    fit_ref[...] = jnp.where(live, fitted_at, 0.0)


def body(kappa_squared, time_coupling, station_value, station_weight, station_cell, slab_blocks):
    n_lon, n_lat, n_tm = (lax.axis_size(axis) for axis in ("lon", "lat", "tm"))
    lats, lons = kappa_squared.shape
    stations = station_value.shape[0]
    hours = HOURS // n_tm
    owners = n_lat * n_tm
    members = n_lon * owners
    padded = -(-(stations // owners) // LANES) * LANES
    slots = owners * padded
    sizes = (n_lon, n_lat, n_tm, hours, lats, lons, stations, padded)
    tall = lats + 2 * PAD
    vmem = pl.BlockSpec(memory_space=pltpu.VMEM)
    dma = pltpu.SemaphoreType.DMA
    field, fit = pl.pallas_call(
        functools.partial(kernel, sizes),
        out_shape=(
            jax.ShapeDtypeStruct((hours, lats, lons), F32),
            jax.ShapeDtypeStruct((1, stations), F32),
        ),
        in_specs=[pl.BlockSpec(memory_space=pl.ANY)] * 5 + [pl.BlockSpec(memory_space=pltpu.SMEM)],
        out_specs=(vmem, vmem),
        scratch_shapes=[
            pltpu.VMEM((hours + 1, tall, lons), F32),
            pltpu.VMEM((hours + 1, tall, lons), F32),
            pltpu.VMEM((hours + 1, lats, lons), F32),
            pltpu.VMEM((hours, tall, lons), F32),
            pltpu.VMEM((hours, lats, lons), F32),
            pltpu.VMEM((hours, lats, lons), F32),
            pltpu.VMEM((hours * lats, slots), BF16),
            pltpu.VMEM((lons, slots), BF16),
            pltpu.VMEM((slots, stations), BF16),
            pltpu.VMEM((owners - 1, 8, padded), F32),
            pltpu.VMEM((owners, 8, padded), F32),
            pltpu.VMEM((owners - 1, 8, padded), F32),
            pltpu.VMEM((owners, 8, padded), F32),
            pltpu.VMEM((2, 4, 2 * hours, lats), F32),
            pltpu.VMEM((2, 16, 2 * hours, lats), F32),
            pltpu.VMEM((2, 4, 2 * hours, lats), F32),
            pltpu.VMEM((4, 8, lats), F32),
            pltpu.VMEM((4, 8, lats), F32),
            pltpu.VMEM((lats, LANES), F32),
            pltpu.VMEM((lats, lons), F32),
            pltpu.VMEM((lats, lons), F32),
            pltpu.VMEM((1, stations), F32),
            pltpu.VMEM((1, stations), F32),
            pltpu.VMEM((3, stations), jnp.int32),
            pltpu.VMEM((4, 1, LANES), F32),
            pltpu.VMEM((4, members - 1, 1, LANES), F32),
            dma((owners - 1,)),
            dma((owners - 1,)),
            dma((owners - 1,)),
            dma((owners - 1,)),
            dma((2, 16)),
            dma((2, 16)),
            dma((2,)),
            dma((2,)),
            dma((4,)),
            dma((4,)),
            dma((5,)),
            dma((2,)),
            dma((2,)),
            dma((4,)),
            dma((4,)),
        ],
        compiler_params=pltpu.CompilerParams(
            collective_id=0, has_side_effects=True, vmem_limit_bytes=VMEM_LIMIT
        ),
    )(
        kappa_squared,
        time_coupling,
        station_value.reshape(1, stations),
        station_weight.reshape(1, stations),
        station_cell,
        slab_blocks,
    )
    return field, fit.reshape(stations)


def solution(mesh):
    rows = P(("groups", "lon", "lat", "tm"))
    return jax.shard_map(
        body,
        mesh=mesh,
        in_specs=(
            P("lat", "lon"),
            P("lat", "lon"),
            rows,
            rows,
            P(None, ("groups", "lon", "lat", "tm")),
            P(("groups", "lon")),
        ),
        out_specs=(P(("groups", "tm"), "lat", "lon"), rows),
        check_vma=False,
    )
```

```python
import functools

import jax
import jax.numpy as jnp
from jax import lax
from jax.experimental import pallas as pl
from jax.experimental.pallas import tpu as pltpu
from jax.sharding import PartitionSpec as P

HOURS = 8
BLOCK = 128
PAD = 8
ROWS = 64
LANES = 128
VMEM_LIMIT = 60 * 1024 * 1024
MESH = pl.DeviceIdType.MESH
F32 = jnp.float32
BF16 = jnp.bfloat16
NT = (((1,), (1,)), ((), ()))


def split(value):
    high = value.astype(BF16)
    return high, (value - high.astype(F32)).astype(BF16)


def dot(left, right, dims=None):
    if dims is None:
        return jnp.dot(left, right, preferred_element_type=F32)
    return lax.dot_general(left, right, dims, preferred_element_type=F32)


def fold(chunk):
    rows, cols = chunk.shape
    summed = jnp.sum(chunk.reshape(rows // 8, 8, cols), axis=0)
    total = summed[:, :LANES]
    for first in range(LANES, cols, LANES):
        total = total + summed[:, first : first + LANES]
    return total


def kernel(
    sizes,
    kappa_hbm,
    tau_hbm,
    value_hbm,
    weight_hbm,
    cell_hbm,
    blocks_ref,
    field_ref,
    fit_ref,
    start_buf,
    image_buf,
    stiff_buf,
    couple_buf,
    second_buf,
    observed_buf,
    row_hot,
    lon_hot,
    slot_hot,
    station_out,
    station_in,
    back_out,
    back_in,
    edge_out,
    edge_in,
    pair_in,
    level_out,
    level_in,
    columns,
    kappa_ref,
    tau_ref,
    value_ref,
    weight_ref,
    cell_ref,
    sum_out,
    sum_in,
    station_send,
    station_recv,
    back_send,
    back_recv,
    edge_send,
    edge_recv,
    pair_send,
    pair_recv,
    level_send,
    level_recv,
    load_sem,
    plane_send,
    plane_recv,
    sum_send,
    sum_recv,
):
    n_lon, n_lat, n_tm, hours, lats, lons, stations, padded = sizes
    owners = n_lat * n_tm
    capacity = stations // owners
    slots = owners * padded
    members = n_lon * owners
    lon, lat, tm = lax.axis_index("lon"), lax.axis_index("lat"), lax.axis_index("tm")
    owner = lat * n_tm + tm
    edge_hour = jnp.where(tm == 0, hours - 1, 0)
    chunks = range(0, lats, ROWS)

    def others(act):
        def at_lon(step_lon, skip):
            to_lon = lon + step_lon
            to_lon = jnp.where(to_lon >= n_lon, to_lon - n_lon, to_lon)
            for step_lat in range(n_lat):
                to_lat = lat + step_lat
                to_lat = jnp.where(to_lat >= n_lat, to_lat - n_lat, to_lat)
                for step_tm in range(n_tm):
                    if skip and step_lat == 0 and step_tm == 0:
                        continue
                    to_tm = tm + step_tm
                    to_tm = jnp.where(to_tm >= n_tm, to_tm - n_tm, to_tm)
                    slot = (step_lon * n_lat + step_lat) * n_tm + step_tm - 1
                    act({"lon": to_lon, "lat": to_lat, "tm": to_tm}, slot)

        at_lon(0, True)
        if n_lon <= 4:
            for step_lon in range(1, n_lon):
                at_lon(step_lon, False)
        else:
            lax.fori_loop(1, n_lon, lambda step, carry: (at_lon(step, False), carry)[1], 0)

    def place_owner(index):
        return {"lon": lon, "lat": lax.div(index, n_tm), "tm": lax.rem(index, n_tm)}

    loads = [
        pltpu.make_async_copy(source, target, load_sem.at[index])
        for index, (source, target) in enumerate(
            [
                (value_hbm, value_ref),
                (weight_hbm, weight_ref),
                (cell_hbm, cell_ref),
                (kappa_hbm, kappa_ref),
                (tau_hbm, tau_ref),
            ]
        )
    ]
    for load in loads:
        load.start()
    barrier = pltpu.get_barrier_semaphore()

    def greet(place, slot):
        pl.semaphore_signal(barrier, inc=1, device_id=place, device_id_type=MESH)

    others(greet)

    for load in loads:
        load.wait()
    zeros = jnp.zeros((6, lats), F32)
    coefficients = (kappa_ref, tau_ref)
    sides = jnp.concatenate(
        [ref[:, lons - 1 : lons] for ref in coefficients]
        + [ref[:, 0:1] for ref in coefficients]
        + [jnp.zeros((lats, LANES - 4), F32)],
        axis=1,
    ).T
    level_out[0] = jnp.concatenate([sides[0:2], zeros], axis=0)
    level_out[1] = jnp.concatenate([sides[2:4], zeros], axis=0)
    zeros = jnp.zeros((6, lons), F32)
    level_out[2] = jnp.concatenate([ref[lats - 1 : lats, :] for ref in coefficients] + [zeros], axis=0)
    level_out[3] = jnp.concatenate([ref[0:1, :] for ref in coefficients] + [zeros], axis=0)
    for ref in (start_buf, image_buf):
        for hour in range(hours):
            ref[hour, 0:PAD, :] = jnp.zeros((PAD, lons), F32)
            ref[hour, PAD + lats :, :] = jnp.zeros((PAD, lons), F32)

    live = lax.broadcasted_iota(jnp.int32, (1, stations), 1) < blocks_ref[0] * BLOCK
    weight = jnp.where(live, weight_ref[...], 0.0)
    lon_at, lat_at, hour_at = cell_ref[0:1, :], cell_ref[1:2, :], cell_ref[2:3, :]
    own_lat = jnp.zeros_like(lat_at)
    for band in range(1, n_lat):
        own_lat = own_lat + (lat_at >= band * lats).astype(jnp.int32)
    own_tm = jnp.zeros_like(lat_at)
    for group in range(1, n_tm):
        own_tm = own_tm + (hour_at >= group * hours).astype(jnp.int32)
    away = own_lat * n_tm + own_tm - owner
    away = jnp.where(away < 0, away + owners, away)
    row_at = (hour_at - own_tm * hours) * lats + lat_at - own_lat * lats
    col_at = lon_at - lon * lons
    kinds = max(16, owners)
    hot = lax.broadcasted_iota(jnp.int32, (kinds, stations), 0) == away
    earlier = lax.broadcasted_iota(jnp.int32, (stations, stations), 0) < lax.broadcasted_iota(
        jnp.int32, (stations, stations), 1
    )
    counts = dot(hot.astype(F32).astype(BF16), earlier.astype(F32).astype(BF16))
    rank = jnp.sum(jnp.where(hot, counts, 0.0), axis=0, keepdims=True).astype(jnp.int32)
    slot = away * padded + rank
    slot_hot[...] = (
        (lax.broadcasted_iota(jnp.int32, (slots, stations), 0) == slot).astype(F32).astype(BF16)
    )
    payload = jnp.concatenate(
        [
            weight,
            weight * value_ref[...],
            row_at.astype(F32),
            col_at.astype(F32),
            jnp.zeros((4, stations), F32),
        ],
        axis=0,
    )
    high, low = split(payload)
    both = dot(jnp.concatenate([high, low], axis=0), slot_hot[...], NT)
    packed = both[:8] + both[8:]
    for step in range(owners):
        chunk = packed[:, step * padded : (step + 1) * padded]
        if step == 0:
            station_in[owners - 1] = chunk
        else:
            station_out[step - 1] = chunk

    lane = lax.broadcasted_iota(jnp.int32, (ROWS, lons), 1)
    lon_up, lon_down = lax.rem(lon + 1, n_lon), lax.rem(lon + n_lon - 1, n_lon)
    lat_up, lat_down = lax.rem(lat + 1, n_lat), lax.rem(lat + n_lat - 1, n_lat)
    pair = lax.rem(tm + 1, n_tm)
    ways = (0, 1, 2, 4, 5) if n_lat == 2 else tuple(range(8))
    slot_of = (0, 1, 2, 2, 4, 5, 4, 5) if n_lat == 2 else tuple(range(8))
    upward = jnp.where(lat == 0, 2, 3) if n_lat == 2 else 2
    targets = (
        (0, lon_up, lat),
        (1, lon_down, lat),
        (upward, lon, lat_up),
        (3, lon, lat_down),
        (upward, lon_up, lat_up),
        (upward, lon_down, lat_up),
        (3, lon_up, lat_down),
        (3, lon_down, lat_down),
    )

    def level_copies():
        copies = []
        for way in ways:
            if way < 4:
                tile, to_lon, to_lat = targets[way]
                copies.append(
                    pltpu.make_async_remote_copy(
                        src_ref=level_out.at[tile],
                        dst_ref=level_in.at[way],
                        send_sem=level_send.at[way],
                        recv_sem=level_recv.at[way],
                        device_id={"lon": to_lon, "lat": to_lat, "tm": tm},
                        device_id_type=MESH,
                    )
                )
        return copies

    pl.semaphore_wait(barrier, members - 1)

    def station_copy(step):
        return pltpu.make_async_remote_copy(
            src_ref=station_out.at[step - 1],
            dst_ref=station_in.at[step - 1],
            send_sem=station_send.at[step - 1],
            recv_sem=station_recv.at[step - 1],
            device_id=place_owner(lax.rem(owner + step, owners)),
            device_id_type=MESH,
        )

    for step in range(1, owners):
        station_copy(step).start()
    for copy in level_copies():
        copy.start()
    for step in range(1, owners):
        station_copy(step).wait()

    arrived = jnp.concatenate([station_in[index] for index in range(owners)], axis=1)
    here_row = arrived[2:3].astype(jnp.int32)
    here_col = arrived[3:4].astype(jnp.int32)
    cells = hours * lats
    row_hot[...] = (
        (lax.broadcasted_iota(jnp.int32, (cells, slots), 0) == here_row).astype(F32).astype(BF16)
    )
    col_mask = lax.broadcasted_iota(jnp.int32, (lons, slots), 0) == here_col
    lon_hot[...] = col_mask.astype(F32).astype(BF16)

    def spread(quantity):
        high, low = split(jnp.where(col_mask, quantity, 0.0))
        return high, low

    weight_high, weight_low = spread(arrived[0:1])
    right_high, right_low = spread(arrived[1:2])

    for hour in range(hours):
        hot_rows = row_hot[hour * lats : (hour + 1) * lats, :]
        start_buf[hour, PAD : PAD + lats, :] = dot(hot_rows, right_high, NT) + dot(
            hot_rows, right_low, NT
        )

    def edge_copies(phase):
        copies = []
        for across in range(2):
            for way in ways:
                tile, to_lon, to_lat = targets[way]
                index = across * 8 + way
                source, target = edge_out.at[phase, tile], edge_in.at[phase, index]
                if way >= 4:
                    half = pl.ds(lons - LANES if way in (4, 6) else 0, LANES)
                    source, target = source.at[:, half], target.at[:, half]
                copies.append(
                    pltpu.make_async_remote_copy(
                        src_ref=source,
                        dst_ref=target,
                        send_sem=edge_send.at[phase, index],
                        recv_sem=edge_recv.at[phase, index],
                        device_id={"lon": to_lon, "lat": to_lat, "tm": pair if across else tm},
                        device_id_type=MESH,
                    )
                )
        copies.append(
            pltpu.make_async_remote_copy(
                src_ref=edge_out.at[phase],
                dst_ref=pair_in.at[phase],
                send_sem=pair_send.at[phase],
                recv_sem=pair_recv.at[phase],
                device_id={"lon": lon, "lat": lat, "tm": pair},
                device_id_type=MESH,
            )
        )
        return copies

    def plane_copy(ref, which):
        return pltpu.make_async_remote_copy(
            src_ref=ref.at[edge_hour, pl.ds(PAD, lats)],
            dst_ref=ref.at[hours, pl.ds(PAD, lats)],
            send_sem=plane_send.at[which],
            recv_sem=plane_recv.at[which],
            device_id={"lon": lon, "lat": lat, "tm": pair},
            device_id_type=MESH,
        )

    def send_edges(ref, phase):
        beside = [
            ref[hour, PAD : PAD + lats, at : at + 1]
            for at in (lons - 2, lons - 1, 0, 1)
            for hour in range(hours)
        ]
        turned = jnp.concatenate(
            beside + [jnp.zeros((lats, LANES - 4 * hours), F32)], axis=1
        ).T
        edge_out[phase, 0] = turned[: 2 * hours]
        edge_out[phase, 1] = turned[2 * hours : 4 * hours]
        for tile, first in ((2, lats - 2), (3, 0)):
            edge_out[phase, tile] = jnp.concatenate(
                [
                    ref[hour, PAD + at : PAD + at + 1, :]
                    for at in (first, first + 1)
                    for hour in range(hours)
                ],
                axis=0,
            )
        for copy in edge_copies(phase):
            copy.start()

    def timeline(own, other, second):
        at = second * hours
        foreign = jnp.where(tm == 0, other[at : at + 1], other[at + hours - 1 : at + hours])
        return jnp.concatenate(
            [
                jnp.where(tm == 0, 0.0, foreign),
                own[at : at + hours],
                jnp.where(tm == 0, foreign, 0.0),
                jnp.zeros((8 - hours - 2, own.shape[1]), F32),
            ],
            axis=0,
        )

    hour_line = lax.broadcasted_iota(jnp.int32, (8, 1), 0)
    at_edge = (hour_line == 1) & (tm == 0) | (hour_line == hours) & (tm == n_tm - 1)

    def outer(far, near, inside, low, high, kappa, tau):
        length = near.shape[1]
        along = lax.broadcasted_iota(jnp.int32, (8, length), 1)
        beside = (
            far
            + inside
            + jnp.where(along == 0, low, pltpu.roll(near, 1, 1))
            + jnp.where(along == length - 1, high, pltpu.roll(near, length - 1, 1))
        )
        stiff = (kappa + 1.0) * near - 0.25 * beside
        diagonal = jnp.where(at_edge, 1.0, 1.0 + tau * tau)
        return diagonal * stiff - tau * (pltpu.roll(stiff, 1, 0) + pltpu.roll(stiff, 7, 0))

    def take_edges(ref, phase):
        for copy in edge_copies(phase):
            copy.wait()
        span = {way: slice(lons - LANES, lons) for way in (4, 6)} | {
            way: slice(0, LANES) for way in (5, 7)
        }
        every = slice(0, lons)
        own = [edge_in[phase, slot_of[way], :, span.get(way, every)] for way in range(8)]
        other = [edge_in[phase, 8 + slot_of[way], :, span.get(way, every)] for way in range(8)]
        lines = {}
        for way in range(8):
            from_below = way in (0, 2, 4, 5)
            lines[way] = timeline(own[way], other[way], 1 if from_below else 0)
            if way < 4:
                lines[way, "far"] = timeline(own[way], other[way], 0 if from_below else 1)
        for way in (2, 4, 5):
            lines[way] = jnp.where(lat == 0, 0.0, lines[way])
        for way in (3, 6, 7):
            lines[way] = jnp.where(lat == n_lat - 1, 0.0, lines[way])
        within = [
            timeline(edge_out[phase, tile], pair_in[phase, tile], second)
            for tile, second in ((1, 0), (0, 1), (3, 0), (2, 1))
        ]
        corner = {
            way: lines[way][:, LANES - 1 :] if way in (4, 6) else lines[way][:, 0:1]
            for way in (4, 5, 6, 7)
        }
        ends = {0: (4, 6), 1: (5, 7), 2: (4, 5), 3: (6, 7)}
        coupled = []
        for way in range(4):
            level = level_in[slot_of[way]]
            low, high = ends[way]
            coupled.append(
                outer(
                    lines[way, "far"],
                    lines[way],
                    within[way],
                    corner[low],
                    corner[high],
                    level[0:1],
                    level[1:2],
                )
            )
        coupled[2] = jnp.where(lat == 0, 0.0, coupled[2])
        coupled[3] = jnp.where(lat == n_lat - 1, 0.0, coupled[3])
        foreign = [
            jnp.where(tm == 0, lines[way][hours + 1 : hours + 2], lines[way][0:1])
            for way in range(4)
        ]
        columns[...] = jnp.concatenate(
            [
                lines[0][1 : hours + 1],
                foreign[0],
                jnp.zeros((7 - hours, lats), F32),
                lines[1][1 : hours + 1],
                foreign[1],
                jnp.zeros((7 - hours, lats), F32),
                coupled[0][1 : hours + 1],
                coupled[1][1 : hours + 1],
                jnp.zeros((LANES - 16 - 2 * hours, lats), F32),
            ],
            axis=0,
        ).T
        ref[hours, PAD - 1 : PAD, :] = foreign[2]
        ref[hours, PAD + lats : PAD + lats + 1, :] = foreign[3]
        for hour in range(hours):
            at = slice(hour + 1, hour + 2)
            stiff_buf[hour, 0:1, :] = stiff_buf[hour, 0:1, :] - 0.25 * lines[2][at]
            stiff_buf[hour, lats - 1 : lats, :] = (
                stiff_buf[hour, lats - 1 : lats, :] - 0.25 * lines[3][at]
            )
            couple_buf[hour, PAD - 1 : PAD, :] = coupled[2][at]
            couple_buf[hour, PAD + lats : PAD + lats + 1, :] = coupled[3][at]

    def stiffen(ref, hour, row, left=None, right=None):
        centre = ref[hour, PAD + row : PAD + row + ROWS, :]
        rows = slice(row, row + ROWS)
        if left is None:
            left, right = 0.0, 0.0
        else:
            left, right = columns[rows, left : left + 1], columns[rows, right : right + 1]
        beside = (
            jnp.where(lane == 0, left, pltpu.roll(centre, 1, 1))
            + jnp.where(lane == lons - 1, right, pltpu.roll(centre, lons - 1, 1))
            + ref[hour, PAD + row - 1 : PAD + row - 1 + ROWS, :]
            + ref[hour, PAD + row + 1 : PAD + row + 1 + ROWS, :]
        )
        return (kappa_ref[rows, :] + 1.0) * centre - 0.25 * beside

    def couple(row):
        rows = slice(row, row + ROWS)
        tau = tau_ref[rows, :]
        inner = 1.0 + tau * tau
        plane = []
        for hour in range(hours):
            beside = jnp.where(
                lane == 0,
                columns[rows, hour : hour + 1],
                jnp.where(lane == lons - 1, columns[rows, 8 + hour : 9 + hour], 0.0),
            )
            plane.append(stiff_buf[hour, rows, :] - 0.25 * beside)
        plane.append(stiff_buf[hours, rows, :])
        for hour in range(hours):
            diagonal = inner
            if hour == 0:
                below = jnp.where(tm == 0, 0.0, plane[hours])
                diagonal = jnp.where(tm == 0, 1.0, inner)
            else:
                below = plane[hour - 1]
            if hour == hours - 1:
                above = jnp.where(tm == n_tm - 1, 0.0, plane[hours])
                diagonal = jnp.where(tm == n_tm - 1, 1.0, inner)
            else:
                above = plane[hour + 1]
            couple_buf[hour, PAD + row : PAD + row + ROWS, :] = diagonal * plane[hour] - tau * (
                below + above
            )

    def sum_start(which, partial):
        sum_out[which] = jnp.sum(partial, axis=0, keepdims=True)

        def send(place, slot):
            pltpu.make_async_remote_copy(
                src_ref=sum_out.at[which],
                dst_ref=sum_in.at[which, slot],
                send_sem=sum_send.at[which],
                recv_sem=sum_recv.at[which],
                device_id=place,
                device_id_type=MESH,
            ).start()

        others(send)

    def sum_finish(which):
        pltpu.make_async_remote_copy(
            src_ref=sum_in.at[which],
            dst_ref=sum_in.at[which],
            send_sem=sum_send.at[which],
            recv_sem=sum_recv.at[which],
            device_id={"lon": lon, "lat": lat, "tm": pair},
            device_id_type=MESH,
        ).wait()
        total = jnp.sum(sum_in[which], axis=0) + sum_out[which]
        return jnp.sum(total, axis=1, keepdims=True)

    def gather(ref):
        picked = jnp.zeros((1, slots), F32)
        for hour in range(hours):
            high, low = split(ref[hour, PAD : PAD + lats, :])
            found = dot(high, lon_hot[...]) + dot(low, lon_hot[...])
            hot_rows = row_hot[hour * lats : (hour + 1) * lats, :].astype(F32)
            picked = picked + jnp.sum(found * hot_rows, axis=0, keepdims=True)
        return picked

    plane_copy(start_buf, 0).start()
    send_edges(start_buf, 0)
    for hour in range(hours):
        hot_rows = row_hot[hour * lats : (hour + 1) * lats, :]
        observed_buf[hour] = dot(hot_rows, weight_high, NT) + dot(hot_rows, weight_low, NT)
    norm_part = jnp.zeros((8, LANES), F32)
    for hour in range(hours):
        for row in chunks:
            chunk = start_buf[hour, PAD + row : PAD + row + ROWS, :]
            norm_part = norm_part + fold(chunk * chunk)
    sum_start(0, norm_part)

    def image(source, target, base, phase, meanwhile):
        for hour in range(hours):
            for row in chunks:
                stiff_buf[hour, row : row + ROWS, :] = stiffen(source, hour, row)
        kept = meanwhile()
        plane_copy(source, phase).wait()
        take_edges(source, phase)
        for row in chunks:
            stiff_buf[hours, row : row + ROWS, :] = stiffen(source, hours, row, hours, 8 + hours)
        for row in chunks:
            couple(row)
        part = jnp.zeros((8, LANES), F32)
        for hour in range(hours):
            for row in chunks:
                at = slice(base + row, base + row + ROWS)
                own = source[hour, PAD + row : PAD + row + ROWS, :]
                result = (
                    stiffen(couple_buf, hour, row, 16 + hour, 16 + hours + hour)
                    + observed_buf[hour, row : row + ROWS, :] * own
                )
                target[hour, at, :] = result
                if phase == 0:
                    part = part + fold(own * result)
        return part, kept

    def first_meanwhile():
        picked = gather(start_buf)
        for copy in level_copies():
            copy.wait()
        return picked

    part, picked_start = image(start_buf, image_buf, PAD, 0, first_meanwhile)
    plane_copy(image_buf, 1).start()
    send_edges(image_buf, 1)
    sum_start(1, part)
    image(image_buf, second_buf, 0, 1, lambda: None)

    norm = sum_finish(0)
    step_first = norm / sum_finish(1)
    part = jnp.zeros((8, LANES), F32)
    for hour in range(hours):
        for row in chunks:
            at = slice(PAD + row, PAD + row + ROWS)
            rest = start_buf[hour, at, :] - step_first * image_buf[hour, at, :]
            couple_buf[hour, at, :] = rest
            part = part + fold(rest * rest)
    sum_start(2, part)

    picked = jnp.concatenate(
        [picked_start, gather(couple_buf), jnp.zeros((6, slots), F32)], axis=0
    )
    for step in range(1, owners + 1):
        chunk = picked[:, (step - 1) * padded : step * padded]
        if step == owners:
            back_in[0] = chunk
        else:
            back_out[step - 1] = chunk

    def back_copy(step):
        return pltpu.make_async_remote_copy(
            src_ref=back_out.at[step - 1],
            dst_ref=back_in.at[step],
            send_sem=back_send.at[step - 1],
            recv_sem=back_recv.at[step - 1],
            device_id=place_owner(lax.rem(owner + owners - step, owners)),
            device_id_type=MESH,
        )

    for step in range(1, owners):
        back_copy(step).start()
    for hour in range(hours):
        for row in chunks:
            at = slice(row, row + ROWS)
            second_buf[hour, at, :] = (
                image_buf[hour, PAD + row : PAD + row + ROWS, :]
                - step_first * second_buf[hour, at, :]
            )
    norm_next = sum_finish(2)
    ratio = norm_next / norm
    part = jnp.zeros((8, LANES), F32)
    for hour in range(hours):
        for row in chunks:
            at = slice(PAD + row, PAD + row + ROWS)
            direction = couple_buf[hour, at, :] + ratio * start_buf[hour, at, :]
            turned = second_buf[hour, row : row + ROWS, :] + ratio * image_buf[hour, at, :]
            couple_buf[hour, at, :] = direction
            part = part + fold(direction * turned)
    sum_start(3, part)

    for step in range(1, owners):
        back_copy(step).wait()
    returned = jnp.concatenate([back_in[index] for index in range(owners)], axis=1)
    high, low = split(returned)
    both = dot(jnp.concatenate([high, low], axis=0), slot_hot[...])
    fitted = both[:8] + both[8:]

    step_second = norm_next / sum_finish(3)
    for hour in range(hours):
        for row in chunks:
            at = slice(PAD + row, PAD + row + ROWS)
            field_ref[hour, row : row + ROWS, :] = (
                step_first * start_buf[hour, at, :] + step_second * couple_buf[hour, at, :]
            )
    fitted_at = step_first * fitted[0:1] + step_second * (fitted[1:2] + ratio * fitted[0:1])
    fit_ref[...] = jnp.where(live, fitted_at, 0.0)


def body(kappa_squared, time_coupling, station_value, station_weight, station_cell, slab_blocks):
    n_lon, n_lat, n_tm = (lax.axis_size(axis) for axis in ("lon", "lat", "tm"))
    lats, lons = kappa_squared.shape
    stations = station_value.shape[0]
    hours = HOURS // n_tm
    owners = n_lat * n_tm
    members = n_lon * owners
    padded = -(-(stations // owners) // LANES) * LANES
    slots = owners * padded
    sizes = (n_lon, n_lat, n_tm, hours, lats, lons, stations, padded)
    tall = lats + 2 * PAD
    vmem = pl.BlockSpec(memory_space=pltpu.VMEM)
    dma = pltpu.SemaphoreType.DMA
    field, fit = pl.pallas_call(
        functools.partial(kernel, sizes),
        out_shape=(
            pltpu.VMEM((hours, lats, lons), F32),
            pltpu.VMEM((1, stations), F32),
        ),
        in_specs=[pl.BlockSpec(memory_space=pl.ANY)] * 5 + [pl.BlockSpec(memory_space=pltpu.SMEM)],
        out_specs=(vmem, vmem),
        scratch_shapes=[
            pltpu.VMEM((hours + 1, tall, lons), F32),
            pltpu.VMEM((hours + 1, tall, lons), F32),
            pltpu.VMEM((hours + 1, lats, lons), F32),
            pltpu.VMEM((hours, tall, lons), F32),
            pltpu.VMEM((hours, lats, lons), F32),
            pltpu.VMEM((hours, lats, lons), F32),
            pltpu.VMEM((hours * lats, slots), BF16),
            pltpu.VMEM((lons, slots), BF16),
            pltpu.VMEM((slots, stations), BF16),
            pltpu.VMEM((owners - 1, 8, padded), F32),
            pltpu.VMEM((owners, 8, padded), F32),
            pltpu.VMEM((owners - 1, 8, padded), F32),
            pltpu.VMEM((owners, 8, padded), F32),
            pltpu.VMEM((2, 4, 2 * hours, lats), F32),
            pltpu.VMEM((2, 16, 2 * hours, lats), F32),
            pltpu.VMEM((2, 4, 2 * hours, lats), F32),
            pltpu.VMEM((4, 8, lats), F32),
            pltpu.VMEM((4, 8, lats), F32),
            pltpu.VMEM((lats, LANES), F32),
            pltpu.VMEM((lats, lons), F32),
            pltpu.VMEM((lats, lons), F32),
            pltpu.VMEM((1, stations), F32),
            pltpu.VMEM((1, stations), F32),
            pltpu.VMEM((3, stations), jnp.int32),
            pltpu.VMEM((4, 1, LANES), F32),
            pltpu.VMEM((4, members - 1, 1, LANES), F32),
            dma((owners - 1,)),
            dma((owners - 1,)),
            dma((owners - 1,)),
            dma((owners - 1,)),
            dma((2, 16)),
            dma((2, 16)),
            dma((2,)),
            dma((2,)),
            dma((4,)),
            dma((4,)),
            dma((5,)),
            dma((2,)),
            dma((2,)),
            dma((4,)),
            dma((4,)),
        ],
        compiler_params=pltpu.CompilerParams(
            collective_id=0, has_side_effects=True, vmem_limit_bytes=VMEM_LIMIT
        ),
    )(
        kappa_squared,
        time_coupling,
        station_value.reshape(1, stations),
        station_weight.reshape(1, stations),
        station_cell,
        slab_blocks,
    )
    return field, fit.reshape(stations)


def solution(mesh):
    rows = P(("groups", "lon", "lat", "tm"))
    return jax.shard_map(
        body,
        mesh=mesh,
        in_specs=(
            P("lat", "lon"),
            P("lat", "lon"),
            rows,
            rows,
            P(None, ("groups", "lon", "lat", "tm")),
            P(("groups", "lon")),
        ),
        out_specs=(P(("groups", "tm"), "lat", "lon"), rows),
        check_vma=False,
    )
```

```python
import functools

import jax
import jax.numpy as jnp
from jax import lax
from jax.experimental import pallas as pl
from jax.experimental.pallas import tpu as pltpu
from jax.sharding import PartitionSpec as P

HOURS = 8
BLOCK = 128
PAD = 8
ROWS = 64
LANES = 128
VMEM_LIMIT = 60 * 1024 * 1024
MESH = pl.DeviceIdType.MESH
F32 = jnp.float32
BF16 = jnp.bfloat16
NT = (((1,), (1,)), ((), ()))


def split(value):
    high = value.astype(BF16)
    return high, (value - high.astype(F32)).astype(BF16)


def dot(left, right, dims=None):
    if dims is None:
        return jnp.dot(left, right, preferred_element_type=F32)
    return lax.dot_general(left, right, dims, preferred_element_type=F32)


def fold(chunk):
    rows, cols = chunk.shape
    summed = jnp.sum(chunk.reshape(rows // 8, 8, cols), axis=0)
    total = summed[:, :LANES]
    for first in range(LANES, cols, LANES):
        total = total + summed[:, first : first + LANES]
    return total


def kernel(
    sizes,
    kappa_hbm,
    tau_hbm,
    value_hbm,
    weight_hbm,
    cell_hbm,
    blocks_ref,
    field_ref,
    fit_ref,
    start_buf,
    image_buf,
    stiff_buf,
    couple_buf,
    second_buf,
    observed_buf,
    row_hot,
    lon_hot,
    slot_hot,
    station_out,
    station_in,
    back_out,
    back_in,
    edge_out,
    edge_in,
    pair_in,
    level_out,
    level_in,
    columns,
    kappa_ref,
    tau_ref,
    value_ref,
    weight_ref,
    cell_ref,
    sum_out,
    sum_in,
    station_send,
    station_recv,
    back_send,
    back_recv,
    edge_send,
    edge_recv,
    pair_send,
    pair_recv,
    level_send,
    level_recv,
    load_sem,
    plane_send,
    plane_recv,
    sum_send,
    sum_recv,
):
    n_lon, n_lat, n_tm, hours, lats, lons, stations, padded = sizes
    owners = n_lat * n_tm
    capacity = stations // owners
    slots = owners * padded
    members = n_lon * owners
    lon, lat, tm = lax.axis_index("lon"), lax.axis_index("lat"), lax.axis_index("tm")
    owner = lat * n_tm + tm
    edge_hour = jnp.where(tm == 0, hours - 1, 0)
    chunks = range(0, lats, ROWS)

    def others(act):
        def at_lon(step_lon, skip):
            to_lon = lon + step_lon
            to_lon = jnp.where(to_lon >= n_lon, to_lon - n_lon, to_lon)
            for step_lat in range(n_lat):
                to_lat = lat + step_lat
                to_lat = jnp.where(to_lat >= n_lat, to_lat - n_lat, to_lat)
                for step_tm in range(n_tm):
                    if skip and step_lat == 0 and step_tm == 0:
                        continue
                    to_tm = tm + step_tm
                    to_tm = jnp.where(to_tm >= n_tm, to_tm - n_tm, to_tm)
                    slot = (step_lon * n_lat + step_lat) * n_tm + step_tm - 1
                    act({"lon": to_lon, "lat": to_lat, "tm": to_tm}, slot)

        at_lon(0, True)
        if n_lon <= 4:
            for step_lon in range(1, n_lon):
                at_lon(step_lon, False)
        else:
            lax.fori_loop(1, n_lon, lambda step, carry: (at_lon(step, False), carry)[1], 0)

    def place_owner(index):
        return {"lon": lon, "lat": lax.div(index, n_tm), "tm": lax.rem(index, n_tm)}

    loads = [
        pltpu.make_async_copy(source, target, load_sem.at[index])
        for index, (source, target) in enumerate(
            [
                (value_hbm, value_ref),
                (weight_hbm, weight_ref),
                (cell_hbm, cell_ref),
                (kappa_hbm, kappa_ref),
                (tau_hbm, tau_ref),
            ]
        )
    ]
    for load in loads:
        load.start()
    barrier = pltpu.get_barrier_semaphore()

    def greet(place, slot):
        pl.semaphore_signal(barrier, inc=1, device_id=place, device_id_type=MESH)

    others(greet)

    for load in loads[:3]:
        load.wait()
    live = lax.broadcasted_iota(jnp.int32, (1, stations), 1) < blocks_ref[0] * BLOCK
    weight = jnp.where(live, weight_ref[...], 0.0)
    lon_at, lat_at, hour_at = cell_ref[0:1, :], cell_ref[1:2, :], cell_ref[2:3, :]
    own_lat = jnp.zeros_like(lat_at)
    for band in range(1, n_lat):
        own_lat = own_lat + (lat_at >= band * lats).astype(jnp.int32)
    own_tm = jnp.zeros_like(lat_at)
    for group in range(1, n_tm):
        own_tm = own_tm + (hour_at >= group * hours).astype(jnp.int32)
    away = own_lat * n_tm + own_tm - owner
    away = jnp.where(away < 0, away + owners, away)
    row_at = (hour_at - own_tm * hours) * lats + lat_at - own_lat * lats
    col_at = lon_at - lon * lons
    kinds = max(16, owners)
    hot = lax.broadcasted_iota(jnp.int32, (kinds, stations), 0) == away
    earlier = lax.broadcasted_iota(jnp.int32, (stations, stations), 0) < lax.broadcasted_iota(
        jnp.int32, (stations, stations), 1
    )
    counts = dot(hot.astype(F32).astype(BF16), earlier.astype(F32).astype(BF16))
    rank = jnp.sum(jnp.where(hot, counts, 0.0), axis=0, keepdims=True).astype(jnp.int32)
    slot = away * padded + rank
    slot_hot[...] = (
        (lax.broadcasted_iota(jnp.int32, (slots, stations), 0) == slot).astype(F32).astype(BF16)
    )
    payload = jnp.concatenate(
        [
            weight,
            weight * value_ref[...],
            row_at.astype(F32),
            col_at.astype(F32),
            jnp.zeros((4, stations), F32),
        ],
        axis=0,
    )
    high, low = split(payload)
    both = dot(jnp.concatenate([high, low], axis=0), slot_hot[...], NT)
    packed = both[:8] + both[8:]
    for step in range(owners):
        chunk = packed[:, step * padded : (step + 1) * padded]
        if step == 0:
            station_in[owners - 1] = chunk
        else:
            station_out[step - 1] = chunk

    lane = lax.broadcasted_iota(jnp.int32, (ROWS, lons), 1)
    lon_up, lon_down = lax.rem(lon + 1, n_lon), lax.rem(lon + n_lon - 1, n_lon)
    lat_up, lat_down = lax.rem(lat + 1, n_lat), lax.rem(lat + n_lat - 1, n_lat)
    pair = lax.rem(tm + 1, n_tm)
    ways = (0, 1, 2, 4, 5) if n_lat == 2 else tuple(range(8))
    slot_of = (0, 1, 2, 2, 4, 5, 4, 5) if n_lat == 2 else tuple(range(8))
    upward = jnp.where(lat == 0, 2, 3) if n_lat == 2 else 2
    targets = (
        (0, lon_up, lat),
        (1, lon_down, lat),
        (upward, lon, lat_up),
        (3, lon, lat_down),
        (upward, lon_up, lat_up),
        (upward, lon_down, lat_up),
        (3, lon_up, lat_down),
        (3, lon_down, lat_down),
    )

    def level_copies():
        copies = []
        for way in ways:
            if way < 4:
                tile, to_lon, to_lat = targets[way]
                copies.append(
                    pltpu.make_async_remote_copy(
                        src_ref=level_out.at[tile],
                        dst_ref=level_in.at[way],
                        send_sem=level_send.at[way],
                        recv_sem=level_recv.at[way],
                        device_id={"lon": to_lon, "lat": to_lat, "tm": tm},
                        device_id_type=MESH,
                    )
                )
        return copies

    pl.semaphore_wait(barrier, members - 1)

    def station_copy(step):
        return pltpu.make_async_remote_copy(
            src_ref=station_out.at[step - 1],
            dst_ref=station_in.at[step - 1],
            send_sem=station_send.at[step - 1],
            recv_sem=station_recv.at[step - 1],
            device_id=place_owner(lax.rem(owner + step, owners)),
            device_id_type=MESH,
        )

    for step in range(1, owners):
        station_copy(step).start()
    for load in loads[3:]:
        load.wait()
    zeros = jnp.zeros((6, lats), F32)
    coefficients = (kappa_ref, tau_ref)
    sides = jnp.concatenate(
        [ref[:, lons - 1 : lons] for ref in coefficients]
        + [ref[:, 0:1] for ref in coefficients]
        + [jnp.zeros((lats, LANES - 4), F32)],
        axis=1,
    ).T
    level_out[0] = jnp.concatenate([sides[0:2], zeros], axis=0)
    level_out[1] = jnp.concatenate([sides[2:4], zeros], axis=0)
    zeros = jnp.zeros((6, lons), F32)
    level_out[2] = jnp.concatenate([ref[lats - 1 : lats, :] for ref in coefficients] + [zeros], axis=0)
    level_out[3] = jnp.concatenate([ref[0:1, :] for ref in coefficients] + [zeros], axis=0)
    for ref in (start_buf, image_buf):
        for hour in range(hours):
            ref[hour, 0:PAD, :] = jnp.zeros((PAD, lons), F32)
            ref[hour, PAD + lats :, :] = jnp.zeros((PAD, lons), F32)
    for copy in level_copies():
        copy.start()
    for step in range(1, owners):
        station_copy(step).wait()

    arrived = jnp.concatenate([station_in[index] for index in range(owners)], axis=1)
    here_row = arrived[2:3].astype(jnp.int32)
    here_col = arrived[3:4].astype(jnp.int32)
    cells = hours * lats
    row_hot[...] = (
        (lax.broadcasted_iota(jnp.int32, (cells, slots), 0) == here_row).astype(F32).astype(BF16)
    )
    col_mask = lax.broadcasted_iota(jnp.int32, (lons, slots), 0) == here_col
    lon_hot[...] = col_mask.astype(F32).astype(BF16)

    def spread(quantity):
        high, low = split(jnp.where(col_mask, quantity, 0.0))
        return high, low

    weight_high, weight_low = spread(arrived[0:1])
    right_high, right_low = spread(arrived[1:2])

    for hour in range(hours):
        hot_rows = row_hot[hour * lats : (hour + 1) * lats, :]
        start_buf[hour, PAD : PAD + lats, :] = dot(hot_rows, right_high, NT) + dot(
            hot_rows, right_low, NT
        )

    def edge_copies(phase):
        copies = []
        for across in range(2):
            for way in ways:
                tile, to_lon, to_lat = targets[way]
                index = across * 8 + way
                source, target = edge_out.at[phase, tile], edge_in.at[phase, index]
                if way >= 4:
                    half = pl.ds(lons - LANES if way in (4, 6) else 0, LANES)
                    source, target = source.at[:, half], target.at[:, half]
                copies.append(
                    pltpu.make_async_remote_copy(
                        src_ref=source,
                        dst_ref=target,
                        send_sem=edge_send.at[phase, index],
                        recv_sem=edge_recv.at[phase, index],
                        device_id={"lon": to_lon, "lat": to_lat, "tm": pair if across else tm},
                        device_id_type=MESH,
                    )
                )
        copies.append(
            pltpu.make_async_remote_copy(
                src_ref=edge_out.at[phase],
                dst_ref=pair_in.at[phase],
                send_sem=pair_send.at[phase],
                recv_sem=pair_recv.at[phase],
                device_id={"lon": lon, "lat": lat, "tm": pair},
                device_id_type=MESH,
            )
        )
        return copies

    def plane_copy(ref, which):
        return pltpu.make_async_remote_copy(
            src_ref=ref.at[edge_hour, pl.ds(PAD, lats)],
            dst_ref=ref.at[hours, pl.ds(PAD, lats)],
            send_sem=plane_send.at[which],
            recv_sem=plane_recv.at[which],
            device_id={"lon": lon, "lat": lat, "tm": pair},
            device_id_type=MESH,
        )

    def send_edges(ref, phase):
        beside = [
            ref[hour, PAD : PAD + lats, at : at + 1]
            for at in (lons - 2, lons - 1, 0, 1)
            for hour in range(hours)
        ]
        turned = jnp.concatenate(
            beside + [jnp.zeros((lats, LANES - 4 * hours), F32)], axis=1
        ).T
        edge_out[phase, 0] = turned[: 2 * hours]
        edge_out[phase, 1] = turned[2 * hours : 4 * hours]
        for tile, first in ((2, lats - 2), (3, 0)):
            edge_out[phase, tile] = jnp.concatenate(
                [
                    ref[hour, PAD + at : PAD + at + 1, :]
                    for at in (first, first + 1)
                    for hour in range(hours)
                ],
                axis=0,
            )
        for copy in edge_copies(phase):
            copy.start()

    def timeline(own, other, second):
        at = second * hours
        foreign = jnp.where(tm == 0, other[at : at + 1], other[at + hours - 1 : at + hours])
        return jnp.concatenate(
            [
                jnp.where(tm == 0, 0.0, foreign),
                own[at : at + hours],
                jnp.where(tm == 0, foreign, 0.0),
                jnp.zeros((8 - hours - 2, own.shape[1]), F32),
            ],
            axis=0,
        )

    hour_line = lax.broadcasted_iota(jnp.int32, (8, 1), 0)
    at_edge = (hour_line == 1) & (tm == 0) | (hour_line == hours) & (tm == n_tm - 1)

    def outer(far, near, inside, low, high, kappa, tau):
        length = near.shape[1]
        along = lax.broadcasted_iota(jnp.int32, (8, length), 1)
        beside = (
            far
            + inside
            + jnp.where(along == 0, low, pltpu.roll(near, 1, 1))
            + jnp.where(along == length - 1, high, pltpu.roll(near, length - 1, 1))
        )
        stiff = (kappa + 1.0) * near - 0.25 * beside
        diagonal = jnp.where(at_edge, 1.0, 1.0 + tau * tau)
        return diagonal * stiff - tau * (pltpu.roll(stiff, 1, 0) + pltpu.roll(stiff, 7, 0))

    def take_edges(ref, phase):
        for copy in edge_copies(phase):
            copy.wait()
        span = {way: slice(lons - LANES, lons) for way in (4, 6)} | {
            way: slice(0, LANES) for way in (5, 7)
        }
        every = slice(0, lons)
        own = [edge_in[phase, slot_of[way], :, span.get(way, every)] for way in range(8)]
        other = [edge_in[phase, 8 + slot_of[way], :, span.get(way, every)] for way in range(8)]
        lines = {}
        for way in range(8):
            from_below = way in (0, 2, 4, 5)
            lines[way] = timeline(own[way], other[way], 1 if from_below else 0)
            if way < 4:
                lines[way, "far"] = timeline(own[way], other[way], 0 if from_below else 1)
        for way in (2, 4, 5):
            lines[way] = jnp.where(lat == 0, 0.0, lines[way])
        for way in (3, 6, 7):
            lines[way] = jnp.where(lat == n_lat - 1, 0.0, lines[way])
        within = [
            timeline(edge_out[phase, tile], pair_in[phase, tile], second)
            for tile, second in ((1, 0), (0, 1), (3, 0), (2, 1))
        ]
        corner = {
            way: lines[way][:, LANES - 1 :] if way in (4, 6) else lines[way][:, 0:1]
            for way in (4, 5, 6, 7)
        }
        ends = {0: (4, 6), 1: (5, 7), 2: (4, 5), 3: (6, 7)}
        coupled = []
        for way in range(4):
            level = level_in[slot_of[way]]
            low, high = ends[way]
            coupled.append(
                outer(
                    lines[way, "far"],
                    lines[way],
                    within[way],
                    corner[low],
                    corner[high],
                    level[0:1],
                    level[1:2],
                )
            )
        coupled[2] = jnp.where(lat == 0, 0.0, coupled[2])
        coupled[3] = jnp.where(lat == n_lat - 1, 0.0, coupled[3])
        foreign = [
            jnp.where(tm == 0, lines[way][hours + 1 : hours + 2], lines[way][0:1])
            for way in range(4)
        ]
        columns[...] = jnp.concatenate(
            [
                lines[0][1 : hours + 1],
                foreign[0],
                jnp.zeros((7 - hours, lats), F32),
                lines[1][1 : hours + 1],
                foreign[1],
                jnp.zeros((7 - hours, lats), F32),
                coupled[0][1 : hours + 1],
                coupled[1][1 : hours + 1],
                jnp.zeros((LANES - 16 - 2 * hours, lats), F32),
            ],
            axis=0,
        ).T
        ref[hours, PAD - 1 : PAD, :] = foreign[2]
        ref[hours, PAD + lats : PAD + lats + 1, :] = foreign[3]
        for hour in range(hours):
            at = slice(hour + 1, hour + 2)
            stiff_buf[hour, 0:1, :] = stiff_buf[hour, 0:1, :] - 0.25 * lines[2][at]
            stiff_buf[hour, lats - 1 : lats, :] = (
                stiff_buf[hour, lats - 1 : lats, :] - 0.25 * lines[3][at]
            )
            couple_buf[hour, PAD - 1 : PAD, :] = coupled[2][at]
            couple_buf[hour, PAD + lats : PAD + lats + 1, :] = coupled[3][at]

    def stiffen(ref, hour, row, left=None, right=None):
        centre = ref[hour, PAD + row : PAD + row + ROWS, :]
        rows = slice(row, row + ROWS)
        if left is None:
            left, right = 0.0, 0.0
        else:
            left, right = columns[rows, left : left + 1], columns[rows, right : right + 1]
        beside = (
            jnp.where(lane == 0, left, pltpu.roll(centre, 1, 1))
            + jnp.where(lane == lons - 1, right, pltpu.roll(centre, lons - 1, 1))
            + ref[hour, PAD + row - 1 : PAD + row - 1 + ROWS, :]
            + ref[hour, PAD + row + 1 : PAD + row + 1 + ROWS, :]
        )
        return (kappa_ref[rows, :] + 1.0) * centre - 0.25 * beside

    def couple(row):
        rows = slice(row, row + ROWS)
        tau = tau_ref[rows, :]
        inner = 1.0 + tau * tau
        plane = []
        for hour in range(hours):
            beside = jnp.where(
                lane == 0,
                columns[rows, hour : hour + 1],
                jnp.where(lane == lons - 1, columns[rows, 8 + hour : 9 + hour], 0.0),
            )
            plane.append(stiff_buf[hour, rows, :] - 0.25 * beside)
        plane.append(stiff_buf[hours, rows, :])
        for hour in range(hours):
            diagonal = inner
            if hour == 0:
                below = jnp.where(tm == 0, 0.0, plane[hours])
                diagonal = jnp.where(tm == 0, 1.0, inner)
            else:
                below = plane[hour - 1]
            if hour == hours - 1:
                above = jnp.where(tm == n_tm - 1, 0.0, plane[hours])
                diagonal = jnp.where(tm == n_tm - 1, 1.0, inner)
            else:
                above = plane[hour + 1]
            couple_buf[hour, PAD + row : PAD + row + ROWS, :] = diagonal * plane[hour] - tau * (
                below + above
            )

    def sum_start(which, partial):
        sum_out[which] = jnp.sum(partial, axis=0, keepdims=True)

        def send(place, slot):
            pltpu.make_async_remote_copy(
                src_ref=sum_out.at[which],
                dst_ref=sum_in.at[which, slot],
                send_sem=sum_send.at[which],
                recv_sem=sum_recv.at[which],
                device_id=place,
                device_id_type=MESH,
            ).start()

        others(send)

    def sum_finish(which):
        pltpu.make_async_remote_copy(
            src_ref=sum_in.at[which],
            dst_ref=sum_in.at[which],
            send_sem=sum_send.at[which],
            recv_sem=sum_recv.at[which],
            device_id={"lon": lon, "lat": lat, "tm": pair},
            device_id_type=MESH,
        ).wait()
        total = jnp.sum(sum_in[which], axis=0) + sum_out[which]
        return jnp.sum(total, axis=1, keepdims=True)

    def gather(ref):
        picked = jnp.zeros((1, slots), F32)
        for hour in range(hours):
            high, low = split(ref[hour, PAD : PAD + lats, :])
            found = dot(high, lon_hot[...]) + dot(low, lon_hot[...])
            hot_rows = row_hot[hour * lats : (hour + 1) * lats, :].astype(F32)
            picked = picked + jnp.sum(found * hot_rows, axis=0, keepdims=True)
        return picked

    plane_copy(start_buf, 0).start()
    send_edges(start_buf, 0)
    for hour in range(hours):
        hot_rows = row_hot[hour * lats : (hour + 1) * lats, :]
        observed_buf[hour] = dot(hot_rows, weight_high, NT) + dot(hot_rows, weight_low, NT)
    norm_part = jnp.zeros((8, LANES), F32)
    for hour in range(hours):
        for row in chunks:
            chunk = start_buf[hour, PAD + row : PAD + row + ROWS, :]
            norm_part = norm_part + fold(chunk * chunk)
    sum_start(0, norm_part)

    def image(source, target, base, phase, meanwhile):
        for hour in range(hours):
            for row in chunks:
                stiff_buf[hour, row : row + ROWS, :] = stiffen(source, hour, row)
        kept = meanwhile()
        plane_copy(source, phase).wait()
        take_edges(source, phase)
        for row in chunks:
            stiff_buf[hours, row : row + ROWS, :] = stiffen(source, hours, row, hours, 8 + hours)
        for row in chunks:
            couple(row)
        part = jnp.zeros((8, LANES), F32)
        for hour in range(hours):
            for row in chunks:
                at = slice(base + row, base + row + ROWS)
                own = source[hour, PAD + row : PAD + row + ROWS, :]
                result = (
                    stiffen(couple_buf, hour, row, 16 + hour, 16 + hours + hour)
                    + observed_buf[hour, row : row + ROWS, :] * own
                )
                target[hour, at, :] = result
                if phase == 0:
                    part = part + fold(own * result)
        return part, kept

    def first_meanwhile():
        picked = gather(start_buf)
        for copy in level_copies():
            copy.wait()
        return picked

    part, picked_start = image(start_buf, image_buf, PAD, 0, first_meanwhile)
    plane_copy(image_buf, 1).start()
    send_edges(image_buf, 1)
    sum_start(1, part)
    image(image_buf, second_buf, 0, 1, lambda: None)

    norm = sum_finish(0)
    step_first = norm / sum_finish(1)
    part = jnp.zeros((8, LANES), F32)
    for hour in range(hours):
        for row in chunks:
            at = slice(PAD + row, PAD + row + ROWS)
            rest = start_buf[hour, at, :] - step_first * image_buf[hour, at, :]
            couple_buf[hour, at, :] = rest
            part = part + fold(rest * rest)
    sum_start(2, part)

    picked = jnp.concatenate(
        [picked_start, gather(couple_buf), jnp.zeros((6, slots), F32)], axis=0
    )
    for step in range(1, owners + 1):
        chunk = picked[:, (step - 1) * padded : step * padded]
        if step == owners:
            back_in[0] = chunk
        else:
            back_out[step - 1] = chunk

    def back_copy(step):
        return pltpu.make_async_remote_copy(
            src_ref=back_out.at[step - 1],
            dst_ref=back_in.at[step],
            send_sem=back_send.at[step - 1],
            recv_sem=back_recv.at[step - 1],
            device_id=place_owner(lax.rem(owner + owners - step, owners)),
            device_id_type=MESH,
        )

    for step in range(1, owners):
        back_copy(step).start()
    for hour in range(hours):
        for row in chunks:
            at = slice(row, row + ROWS)
            second_buf[hour, at, :] = (
                image_buf[hour, PAD + row : PAD + row + ROWS, :]
                - step_first * second_buf[hour, at, :]
            )
    norm_next = sum_finish(2)
    ratio = norm_next / norm
    part = jnp.zeros((8, LANES), F32)
    for hour in range(hours):
        for row in chunks:
            at = slice(PAD + row, PAD + row + ROWS)
            direction = couple_buf[hour, at, :] + ratio * start_buf[hour, at, :]
            turned = second_buf[hour, row : row + ROWS, :] + ratio * image_buf[hour, at, :]
            couple_buf[hour, at, :] = direction
            part = part + fold(direction * turned)
    sum_start(3, part)

    for step in range(1, owners):
        back_copy(step).wait()
    returned = jnp.concatenate([back_in[index] for index in range(owners)], axis=1)
    high, low = split(returned)
    both = dot(jnp.concatenate([high, low], axis=0), slot_hot[...])
    fitted = both[:8] + both[8:]

    step_second = norm_next / sum_finish(3)
    for hour in range(hours):
        for row in chunks:
            at = slice(PAD + row, PAD + row + ROWS)
            field_ref[hour, row : row + ROWS, :] = (
                step_first * start_buf[hour, at, :] + step_second * couple_buf[hour, at, :]
            )
    fitted_at = step_first * fitted[0:1] + step_second * (fitted[1:2] + ratio * fitted[0:1])
    fit_ref[...] = jnp.where(live, fitted_at, 0.0)


def body(kappa_squared, time_coupling, station_value, station_weight, station_cell, slab_blocks):
    n_lon, n_lat, n_tm = (lax.axis_size(axis) for axis in ("lon", "lat", "tm"))
    lats, lons = kappa_squared.shape
    stations = station_value.shape[0]
    hours = HOURS // n_tm
    owners = n_lat * n_tm
    members = n_lon * owners
    padded = -(-(stations // owners) // LANES) * LANES
    slots = owners * padded
    sizes = (n_lon, n_lat, n_tm, hours, lats, lons, stations, padded)
    tall = lats + 2 * PAD
    vmem = pl.BlockSpec(memory_space=pltpu.VMEM)
    dma = pltpu.SemaphoreType.DMA
    field, fit = pl.pallas_call(
        functools.partial(kernel, sizes),
        out_shape=(
            pltpu.VMEM((hours, lats, lons), F32),
            pltpu.VMEM((1, stations), F32),
        ),
        in_specs=[pl.BlockSpec(memory_space=pl.ANY)] * 5 + [pl.BlockSpec(memory_space=pltpu.SMEM)],
        out_specs=(vmem, vmem),
        scratch_shapes=[
            pltpu.VMEM((hours + 1, tall, lons), F32),
            pltpu.VMEM((hours + 1, tall, lons), F32),
            pltpu.VMEM((hours + 1, lats, lons), F32),
            pltpu.VMEM((hours, tall, lons), F32),
            pltpu.VMEM((hours, lats, lons), F32),
            pltpu.VMEM((hours, lats, lons), F32),
            pltpu.VMEM((hours * lats, slots), BF16),
            pltpu.VMEM((lons, slots), BF16),
            pltpu.VMEM((slots, stations), BF16),
            pltpu.VMEM((owners - 1, 8, padded), F32),
            pltpu.VMEM((owners, 8, padded), F32),
            pltpu.VMEM((owners - 1, 8, padded), F32),
            pltpu.VMEM((owners, 8, padded), F32),
            pltpu.VMEM((2, 4, 2 * hours, lats), F32),
            pltpu.VMEM((2, 16, 2 * hours, lats), F32),
            pltpu.VMEM((2, 4, 2 * hours, lats), F32),
            pltpu.VMEM((4, 8, lats), F32),
            pltpu.VMEM((4, 8, lats), F32),
            pltpu.VMEM((lats, LANES), F32),
            pltpu.VMEM((lats, lons), F32),
            pltpu.VMEM((lats, lons), F32),
            pltpu.VMEM((1, stations), F32),
            pltpu.VMEM((1, stations), F32),
            pltpu.VMEM((3, stations), jnp.int32),
            pltpu.VMEM((4, 1, LANES), F32),
            pltpu.VMEM((4, members - 1, 1, LANES), F32),
            dma((owners - 1,)),
            dma((owners - 1,)),
            dma((owners - 1,)),
            dma((owners - 1,)),
            dma((2, 16)),
            dma((2, 16)),
            dma((2,)),
            dma((2,)),
            dma((4,)),
            dma((4,)),
            dma((5,)),
            dma((2,)),
            dma((2,)),
            dma((4,)),
            dma((4,)),
        ],
        compiler_params=pltpu.CompilerParams(
            collective_id=0, has_side_effects=True, vmem_limit_bytes=VMEM_LIMIT
        ),
    )(
        kappa_squared,
        time_coupling,
        station_value.reshape(1, stations),
        station_weight.reshape(1, stations),
        station_cell,
        slab_blocks,
    )
    return field, fit.reshape(stations)


def solution(mesh):
    rows = P(("groups", "lon", "lat", "tm"))
    return jax.shard_map(
        body,
        mesh=mesh,
        in_specs=(
            P("lat", "lon"),
            P("lat", "lon"),
            rows,
            rows,
            P(None, ("groups", "lon", "lat", "tm")),
            P(("groups", "lon")),
        ),
        out_specs=(P(("groups", "tm"), "lat", "lon"), rows),
        check_vma=False,
    )
```
